128 devices in a mesh: ctx: 8 (over z, x_lo), exp: 16 (over y, x_hi, core).
Axes of the slice: x: 4 (x_hi: 2, x_lo: 2; x = x_hi * 2 + x_lo), y: 4, z: 4, core: 2. Of those that a mesh axis runs over, the one named last changes fastest.
Arguments:
- queries: bfloat16 [1024, 6144], P('ctx', 'exp'), may hold values from -8 to 8
- keys_values: bfloat16 [2, 1024, 1024], P(None, 'ctx', 'exp'), may hold values from -8 to 8
- residual: bfloat16 [1024, 6144], P(('ctx', 'exp')), may hold values from -12 to 12
- out_weight: bfloat16 [6144, 6144], P('exp', 'ctx'), may hold values from -0.078125 to 0.078125
- norm_gain: float32 [6144], replicated, may hold values from 0.5 to 2
- routes: int32 [1024, 4], P(('ctx', 'exp')), may hold values from 0 to 15, as said below
- route_weight: float32 [1024, 4], P(('ctx', 'exp')), may hold values from 0.1 to 1
- gate_weight: bfloat16 [16, 6144, 5376], P('exp', None, 'ctx'), may hold values from -0.078125 to 0.078125
- up_weight: bfloat16 [16, 6144, 5376], P('exp', None, 'ctx'), may hold values from -0.078125 to 0.078125
- down_weight: bfloat16 [16, 5376, 6144], P('exp', 'ctx'), may hold values from -0.078125 to 0.078125
Outputs:
- layer_out: bfloat16 [1024, 6144], P(('ctx', 'exp'))
The draws below stay inside these ranges and needn't reach their ends.
Inputs may be any that keep to these rules, and one draw needn't show every extreme that they name: `routes`: each row names 4 different experts. Within each aligned block of 8 rows (the rows of one device) no expert is named by more than 4 rows, and one expert is named by exactly 4 rows in every block.
All inputs are finite; a program needn't handle non-finite values.
Results may differ from the reference program's by a relative error of at most 0.025.
Values may be sent and summed in bfloat16 or wider, within the bound.
A program may use at most 128 MiB of HBM per device.

```python
import math
import jax
import jax.numpy as jnp
from jax import lax

D = 6144
HD = 128
GROUP = 6
FF = 5376
TOP = 4
TOK_DEV = 8
SEQ = 1024
KV_HEADS = 8
HEADS = 48
EXPERTS = 16
CAP = 4
N_CTX = 8
N_EXP = 16


def draw_queries(key, part):
    key = jax.random.fold_in(key, 7)
    base_draw = 1.5 * jax.random.truncated_normal(key, -4.0, 4.0, (SEQ, HEADS, HD), jnp.float32)
    return base_draw.reshape(SEQ, HEADS * HD).astype(jnp.bfloat16)


def draw_keys_values(key, part):
    key = jax.random.fold_in(key, 8)
    key_part, value_part = jax.random.split(key)
    keys = jax.random.truncated_normal(key_part, -4.0, 4.0, (SEQ, KV_HEADS, HD), jnp.float32)
    values = 2.0 * jax.random.truncated_normal(value_part, -4.0, 4.0, (SEQ, KV_HEADS, HD), jnp.float32)
    stacked = jnp.stack([keys.reshape(SEQ, KV_HEADS * HD), values.reshape(SEQ, KV_HEADS * HD)])
    return stacked.astype(jnp.bfloat16)


def draw_residual(key, part):
    key = jax.random.fold_in(key, 9)
    keys_list = jax.random.split(key, 3)
    column_scale = jnp.exp(jax.random.uniform(keys_list[0], (D,), jnp.float32, math.log(0.1), 0.0))
    row_scale = jnp.exp(jax.random.uniform(keys_list[1], (SEQ,), jnp.float32, math.log(0.3), math.log(3.0)))
    base_draw = jax.random.truncated_normal(keys_list[2], -4.0, 4.0, (SEQ, D), jnp.float32)
    return (base_draw * column_scale[None, :] * row_scale[:, None]).astype(jnp.bfloat16)


def draw_routes(key, part):
    key = jax.random.fold_in(key, 10)
    hot_key, block_key = jax.random.split(key)
    hot_expert = jax.random.randint(hot_key, (), 0, EXPERTS).astype(jnp.int32)
    block_keys = jax.random.split(block_key, SEQ // TOK_DEV)

    def one_block(single_key):
        key_rank, key_place, key_order, key_begin = jax.random.split(single_key, 4)
        rank = jax.random.permutation(key_rank, TOK_DEV).astype(jnp.int32)
        has_hot = (rank < CAP).astype(jnp.int32)
        hot_place = jax.random.randint(key_place, (TOK_DEV,), 0, TOP).astype(jnp.int32)
        others = jax.random.permutation(key_order, EXPERTS - 1).astype(jnp.int32)
        begin = jax.random.randint(key_begin, (), 0, EXPERTS - 1).astype(jnp.int32)
        per_row = TOP - has_hot
        before = jnp.cumsum(per_row) - per_row
        choice_index = jnp.arange(TOP, dtype=jnp.int32)[None, :]
        shifted = choice_index - has_hot[:, None] * (choice_index > hot_place[:, None]).astype(jnp.int32)
        counter = before[:, None] + shifted
        other_ids = (hot_expert + 1 + others[(begin + counter) % (EXPERTS - 1)]) % EXPERTS
        is_hot = (has_hot[:, None] == 1) & (choice_index == hot_place[:, None])
        return jnp.where(is_hot, hot_expert, other_ids).astype(jnp.int32)
    return jax.vmap(one_block)(block_keys).reshape(SEQ, TOP).astype(jnp.int32)


def shard_levels(stream_key, shape, cuts, smallest, high):
    loudness, own = 1.0, jax.random.fold_in(stream_key, 6)
    for position, shards_of in cuts:
        draws = jnp.exp(jax.random.uniform(jax.random.fold_in(own, position), (shards_of,), jnp.float32, smallest / len(cuts), high / len(cuts)))
        loudness = loudness * jnp.repeat(draws, shape[position] // shards_of).reshape([-1 if axis == position else 1 for axis in range(len(shape))])
    return loudness


def bell_draw(stream_key, dims, deviation, most, cuts=(), kind=jnp.bfloat16):
    result = jax.random.normal(stream_key, dims, jnp.float32) * deviation
    if len(cuts) > 0:
        result = shard_levels(stream_key, dims, cuts, -0.22, 0.18) * result
    return jnp.clip(result, min=-most, max=most).astype(kind)


def setup_inputs(seed: int = 0) -> dict:
    splits = jax.random.split(jax.random.key(seed), 11)
    return {
        "queries": draw_queries(jax.random.fold_in(splits[10], 71), 0),
        "keys_values": draw_keys_values(jax.random.fold_in(splits[10], 71), 0),
        "residual": draw_residual(jax.random.fold_in(splits[10], 71), 0),
        "out_weight": bell_draw(splits[3], (HEADS * HD, D), (HEADS * HD) ** -0.5, 0.078125, ((0, 16), (1, 8))),
        "norm_gain": jnp.clip(jnp.exp(jax.random.uniform(splits[4], (D,), jnp.float32, math.log(0.5), math.log(2.0))), 0.5, 2.0),
        "routes": draw_routes(jax.random.fold_in(splits[10], 71), 0),
        "route_weight": jnp.clip(0.1 + 0.9 * jax.random.uniform(splits[6], (SEQ, TOP), jnp.float32) ** shard_levels(splits[6], (SEQ, TOP), ((0, 128),), -0.2, 0.2), 0.1, 1.0),
        "gate_weight": bell_draw(splits[7], (EXPERTS, D, FF), D ** -0.5, 0.078125, ((0, 16), (2, 8))),
        "up_weight": bell_draw(splits[8], (EXPERTS, D, FF), D ** -0.5, 0.078125, ((0, 16), (2, 8))),
        "down_weight": bell_draw(splits[9], (EXPERTS, FF, D), FF ** -0.5, 0.078125, ((0, 16), (1, 8))),
    }


def attend_head(query_block, key_block, value_block, causal):
    scores = jnp.dot(query_block, key_block.T, preferred_element_type=jnp.float32) / math.sqrt(HD)
    masked = jnp.where(causal, scores, -jnp.inf)
    weights = jnp.exp(masked - lax.optimization_barrier(jnp.max(masked, axis=1, keepdims=True)))
    weights = weights / lax.optimization_barrier(jnp.sum(weights, axis=1, keepdims=True))
    return jnp.dot(weights, value_block.astype(jnp.float32), precision=lax.Precision.HIGHEST)

def reference(queries, keys_values, residual, out_weight, norm_gain, routes, route_weight, gate_weight, up_weight, down_weight):
    query_heads = queries.reshape(SEQ, HEADS, HD)
    key_heads = keys_values[0].reshape(SEQ, KV_HEADS, HD)
    value_heads = keys_values[1].reshape(SEQ, KV_HEADS, HD)
    positions = jnp.arange(SEQ, dtype=jnp.int32)
    causal = positions[:, None] >= positions[None, :]

    def one_head(head_index):
        group_index = head_index // GROUP
        return attend_head(query_heads[:, head_index], key_heads[:, group_index], value_heads[:, group_index], causal)
    heads_out = lax.map(one_head, jnp.arange(HEADS, dtype=jnp.int32))
    attended = jnp.transpose(heads_out, (1, 0, 2)).reshape(SEQ, HEADS * HD).astype(jnp.bfloat16)
    projected = jnp.dot(attended, out_weight, preferred_element_type=jnp.float32)
    hidden_state = residual.astype(jnp.float32) + projected
    row_mean = lax.optimization_barrier(jnp.mean(hidden_state, axis=1, keepdims=True))
    centered = hidden_state - row_mean
    variance = lax.optimization_barrier(jnp.mean(centered * centered, axis=1, keepdims=True))
    normed = (centered * lax.rsqrt(variance + 1e-05) * norm_gain).astype(jnp.bfloat16)
    limit = CAP * N_CTX * N_EXP
    pair_count = SEQ * TOP
    flat_routes = routes.reshape(-1)
    flat_weight = route_weight.reshape(-1)
    slice_width = FF // N_CTX

    def add_expert(combined, expert_index):
        pairs = jnp.nonzero(flat_routes == expert_index, size=limit, fill_value=pair_count)[0].astype(jnp.int32)
        token_index = pairs // TOP
        token_block = normed[jnp.minimum(token_index, SEQ - 1)]
        gate_part = jnp.dot(token_block, gate_weight[expert_index], preferred_element_type=jnp.float32)
        up_part = jnp.dot(token_block, up_weight[expert_index], preferred_element_type=jnp.float32)
        activated = (jax.nn.silu(gate_part) * up_part).astype(jnp.bfloat16)
        pieces = jnp.einsum('rcf,cfd->crd', activated.reshape(limit, N_CTX, slice_width).astype(jnp.float32), down_weight[expert_index].reshape(N_CTX, slice_width, D).astype(jnp.float32), precision=lax.Precision.HIGHEST)
        pieces = lax.optimization_barrier(pieces.astype(jnp.bfloat16)).astype(jnp.float32)
        expert_out = lax.optimization_barrier(jnp.sum(pieces, axis=0))
        gate_values = flat_weight[jnp.minimum(pairs, pair_count - 1)]
        combined = combined.at[token_index].add(gate_values[:, None] * expert_out, mode='drop')
        return (combined, None)
    combined, unused = lax.scan(add_expert, jnp.zeros((SEQ, D), jnp.float32), jnp.arange(EXPERTS, dtype=jnp.int32))
    return (hidden_state + combined).astype(jnp.bfloat16)
```

```python
import math

import jax
import jax.numpy as jnp
from jax import lax
from jax.experimental import pallas as pl
from jax.experimental.pallas import tpu as pltpu
from jax.sharding import PartitionSpec as P

HD = 128


def from_partner(value, axis, bit):
    return lax.ppermute(value, axis, [(i, i ^ 1 << bit) for i in range(lax.axis_size(axis))])


MESH = pl.DeviceIdType.MESH
ORDERS = (("x", "y", "z"), ("y", "z", "x"), ("z", "x", "y"))
OFFSETS = (0, -1, 1, 2)
GROUPS_BACK = (2, 1, -1, 0)


def place():
    ctx = lax.axis_index("ctx")
    exp = lax.axis_index("exp")
    return {
        "z": ctx // 2,
        "x": ((exp // 2) % 2) * 2 + ctx % 2,
        "y": exp // 4,
        "k": exp % 2,
    }


def device_at(at):
    return (at["z"] * 2 + at["x"] % 2, at["y"] * 4 + (at["x"] // 2) * 2 + at["k"])


def moved(at, axis, by):
    there = dict(at)
    if axis == "k":
        there["k"] = 1 - at["k"]
    else:
        there[axis] = (at[axis] + by + 4) % 4
    return there


def send(source, target, send_sem, recv_sem, device):
    copy = pltpu.make_async_remote_copy(
        src_ref=source,
        dst_ref=target,
        send_sem=send_sem,
        recv_sem=recv_sem,
        device_id=device,
        device_id_type=MESH,
    )
    copy.start()
    return copy


def arrived(target, send_sem, recv_sem, device):
    pltpu.make_async_remote_copy(
        src_ref=target,
        dst_ref=target,
        send_sem=send_sem,
        recv_sem=recv_sem,
        device_id=device,
        device_id_type=MESH,
    ).wait_recv()


def expert_kernel(
    piece_ref,
    hidden_ref,
    pick_ref,
    slot_ref,
    share_ref,
    gate_hbm,
    up_hbm,
    down_hbm,
    out_ref,
    gate,
    up,
    down,
    rows,
    relay3,
    full3,
    relay2,
    full2,
    relay1,
    full1,
    gate_sum,
    up_sum,
    mixed,
    mixed_other,
    load_sem,
    s1,
    r1,
    s2,
    r2,
    s3,
    r3,
    sp,
    rp,
    sd,
    rd,
    bs3,
    br3,
    bs2,
    br2,
    bs1,
    br1,
):
    at = place()
    k = at["k"]
    near = {(a, d): device_at(moved(at, a, d)) for a in "xyz" for d in (1, -1)}
    partner = device_at(moved(at, "k", 1))

    barrier = pltpu.get_barrier_semaphore()
    for device in [*near.values(), partner]:
        pl.semaphore_signal(barrier, inc=1, device_id=device, device_id_type=MESH)
    pl.semaphore_wait(barrier, 7)

    def ring(axis, by):
        return (at[axis] + by + 4) % 4

    def piece(q, d):
        a1, a2, a3 = ORDERS[q]
        return rows.at[k, q, at[a3], at[a2], ring(a1, d)]

    def line(q, d):
        a1, a2, a3 = ORDERS[q]
        return rows.at[k, q, at[a3], ring(a2, d)]

    def group(q, d, g):
        a1, a2, a3 = ORDERS[q]
        return rows.at[k, q, ring(a3, d), ring(a2, g)]

    def group_other(q, d, g):
        a1, a2, a3 = ORDERS[q]
        return rows.at[1 - k, q, ring(a3, d), ring(a2, g)]

    sent = []

    def go(*args):
        sent.append(send(*args))

    for q in range(3):
        a1 = ORDERS[q][0]
        piece(q, 0)[...] = piece_ref[q]
        for kind, d in ((0, 1), (1, -1)):
            go(piece(q, 0), piece(q, 0), s1.at[q, kind], r1.at[q, kind], near[a1, d])

    loads = [
        pltpu.make_async_copy(gate_hbm.at[0], gate, load_sem.at[0]),
        pltpu.make_async_copy(up_hbm.at[0], up, load_sem.at[1]),
        pltpu.make_async_copy(down_hbm.at[0], down.at[0], load_sem.at[2]),
    ]
    for load in loads:
        load.start()
    go(down_hbm.at[0], down.at[1], sd.at[0], rd.at[0], partner)
    gate_sum[...] = jnp.zeros_like(gate_sum)
    up_sum[...] = jnp.zeros_like(up_sum)

    def half(ref, index, width):
        return ref.at[pl.ds(index * width, width)]

    def relay(q, axis, whole, kind, width, ssem, rsem):
        d = 1 if kind == 0 else -1
        arrived(whole(-d), ssem[kind], rsem[kind], near[axis, -d])
        part = half(whole(-d), kind, width)
        go(part, part, ssem[2 + kind], rsem[2 + kind], near[axis, d])

    def finish(q, axis, whole, width, ssem, rsem):
        for kind in (0, 1):
            d = 1 if kind == 0 else -1
            arrived(half(whole(2), kind, width), ssem[2 + kind], rsem[2 + kind], near[axis, -d])

    def sems(ref, *index):
        return [ref.at[(*index, kind)] for kind in range(4)]

    def to_ring(axis, whole, ssem, rsem):
        for kind, d in ((0, 1), (1, -1)):
            go(whole(0), whole(0), ssem[kind], rsem[kind], near[axis, d])

    def forward(q, d, g):
        go(group(q, d, g), group(q, d, g), sp.at[q, d % 4, g % 4], rp.at[q, d % 4, g % 4], partner)

    def one_plane(q, g):
        a3 = ORDERS[q][2]
        return a3, (lambda d: group(q, d, g)), sems(s3, q, g % 4), sems(r3, q, g % 4)

    for kind in (0, 1):
        for q in range(3):
            relay(q, ORDERS[q][0], lambda d: piece(q, d), kind, 1, sems(s1, q), sems(r1, q))
    for q in range(3):
        a1, a2, a3 = ORDERS[q]
        finish(q, a1, lambda d: piece(q, d), 1, sems(s1, q), sems(r1, q))
        to_ring(a2, lambda d: line(q, d), sems(s2, q), sems(r2, q))
        to_ring(*one_plane(q, 0))
        forward(q, 0, 0)
    for kind in (0, 1):
        g = -1 if kind == 0 else 1
        for q in range(3):
            a1, a2, a3 = ORDERS[q]
            relay(q, a2, lambda d: line(q, d), kind, 2, sems(s2, q), sems(r2, q))
            to_ring(*one_plane(q, g))
            forward(q, 0, g)
    for q in range(3):
        a1, a2, a3 = ORDERS[q]
        finish(q, a2, lambda d: line(q, d), 2, sems(s2, q), sems(r2, q))
        to_ring(*one_plane(q, 2))
        forward(q, 0, 2)

    def index_of(q, i3, i2):
        a1, a2, a3 = ORDERS[q]
        where = {a3: i3, a2: i2, a1: slice(None)}
        return where["z"], where["y"], where["x"]

    def hidden_unit(q, d):
        a1, a2, a3 = ORDERS[q]
        for g in OFFSETS:
            arrived(
                group_other(q, d, g), sp.at[q, d % 4, g % 4], rp.at[q, d % 4, g % 4], partner
            )
        i3 = ring(a3, d)
        number = lax.broadcasted_iota(jnp.int32, (256, 512), 0)
        picker = jnp.where(number == pick_ref[q, i3], 1.0, 0.0).astype(jnp.bfloat16)
        picked = []
        for s in range(2):
            both = jnp.concatenate(
                [rows[c, q, i3, :, :, s].reshape(256, 512) for c in range(2)], axis=0
            )
            picked.append(
                jnp.dot(picker, both, preferred_element_type=jnp.float32).astype(jnp.bfloat16)
            )
        for weight, total in ((gate, gate_sum), (up, up_sum)):
            value = None
            for h in range(2):
                x = jnp.concatenate([p[h * 128 : h * 128 + 128] for p in picked], axis=1)
                base = h * 3072 + q * 1024
                term = jnp.dot(
                    x, weight[base : base + 1024, :], preferred_element_type=jnp.float32
                )
                value = term if value is None else value + term
            for i2 in range(4):
                where = index_of(q, i3, i2)
                total[where] += value[i2 * 32 : i2 * 32 + 32].reshape(4, 8, 672)

    for t, g in enumerate(OFFSETS):
        for q in range(3):
            a3, whole, ssem, rsem = one_plane(q, g)
            for kind in (0, 1):
                relay(q, a3, whole, kind, 2, ssem, rsem)
                forward(q, -1 if kind == 0 else 1, g)
        if t == 0:
            loads[0].wait()
            loads[1].wait()
        if t >= 1:
            hidden_unit(t - 1, 0)
    for t, g in enumerate(OFFSETS):
        for q in range(3):
            a3, whole, ssem, rsem = one_plane(q, g)
            finish(q, a3, whole, 2, ssem, rsem)
            forward(q, 2, g)
        if t == 0:
            for q in range(3):
                hidden_unit(q, -1)
        if t == 1:
            for q in range(3):
                hidden_unit(q, 1)
    for q in range(3):
        hidden_unit(q, 2)

    number = lax.broadcasted_iota(jnp.int32, (256, 128), 1)
    for z in range(4):
        g = gate_sum[z].reshape(128, 672)
        u = up_sum[z].reshape(128, 672)
        activated = (g / (1.0 + jnp.exp(-g)) * u).astype(jnp.bfloat16)
        spread = jnp.where(number == slot_ref[z], 1.0, 0.0).astype(jnp.bfloat16)
        value = jnp.dot(spread, activated, preferred_element_type=jnp.float32) * share_ref[z]
        mixed[0, z] = value[:128].astype(jnp.bfloat16)
        mixed[1, z] = value[128:].astype(jnp.bfloat16)
    go(mixed.at[1 - k], mixed_other, sd.at[1], rd.at[1], partner)
    gate_sum[...] = mixed[k].astype(jnp.float32).reshape(4, 4, 4, 8, 672)
    loads[2].wait()
    arrived(down.at[1], sd.at[0], rd.at[0], partner)
    arrived(mixed_other, sd.at[1], rd.at[1], partner)
    up_sum[...] = mixed_other[...].astype(jnp.float32).reshape(4, 4, 4, 8, 672)
    for copy in sent:
        copy.wait_send()
    sent.clear()

    def down_unit(q, d):
        i3 = ring(ORDERS[q][2], d)
        a = [
            jnp.concatenate(
                [total[index_of(q, i3, i2)].reshape(32, 672) for i2 in range(4)], axis=0
            ).astype(jnp.bfloat16)
            for total in (gate_sum, up_sum)
        ]
        for s in range(2):
            sides = []
            for h in range(2):
                base = h * 3072 + q * 1024 + s * 512
                value = jnp.dot(
                    a[0], down[0, :, base : base + 512], preferred_element_type=jnp.float32
                ) + jnp.dot(
                    a[1], down[1, :, base : base + 512], preferred_element_type=jnp.float32
                )
                sides.append(value.reshape(16, 8, 512))
            joined = jnp.concatenate(sides, axis=1).astype(jnp.bfloat16)
            rows[k, q, i3, :, :, s] = joined.reshape(4, 4, 16, 512)

    def add_into(ref, *others):
        value = ref[...].astype(jnp.float32)
        for other in others:
            value = value + other[...].astype(jnp.float32)
        ref[...] = value.astype(jnp.bfloat16)

    def first(axis, far, width, slots, ssem, rsem):
        for kind, d in ((0, 1), (1, -1)):
            go(half(far, kind, width), slots[kind], ssem[kind], rsem[kind], near[axis, d])

    def second(axis, whole, width, slots, full, ssem, rsem):
        for kind, d in ((0, 1), (1, -1)):
            arrived(slots[kind], ssem[kind], rsem[kind], near[axis, -d])
            add_into(half(whole(d), kind, width), slots[kind])
            go(whole(d), full[kind], ssem[2 + kind], rsem[2 + kind], near[axis, d])

    def third(axis, whole, full, ssem, rsem):
        for kind, d in ((0, 1), (1, -1)):
            arrived(full[kind], ssem[2 + kind], rsem[2 + kind], near[axis, -d])
        add_into(whole(0), *full)

    def pair(ref, *index):
        return [ref.at[(*index, kind)] for kind in range(2)]

    for q in range(3):
        down_unit(q, 2)
        for g in GROUPS_BACK:
            first(
                ORDERS[q][2],
                group(q, 2, g),
                2,
                pair(relay3, q, g % 4),
                sems(bs3, q, g % 4),
                sems(br3, q, g % 4),
            )
    for q in range(3):
        down_unit(q, 1)
        down_unit(q, -1)
        for g in GROUPS_BACK:
            second(
                ORDERS[q][2],
                lambda d: group(q, d, g),
                2,
                pair(relay3, q, g % 4),
                pair(full3, q, g % 4),
                sems(bs3, q, g % 4),
                sems(br3, q, g % 4),
            )
    for q in range(3):
        down_unit(q, 0)

    def args2(q):
        return ORDERS[q][1], (lambda d: line(q, d)), sems(bs2, q), sems(br2, q)

    for g in GROUPS_BACK:
        for q in range(3):
            third(
                ORDERS[q][2],
                lambda d: group(q, d, g),
                pair(full3, q, g % 4),
                sems(bs3, q, g % 4),
                sems(br3, q, g % 4),
            )
            if g == 2:
                first(
                    ORDERS[q][1], line(q, 2), 2, pair(relay2, q), sems(bs2, q), sems(br2, q)
                )
        if g == -1:
            for q in range(3):
                axis, whole, ssem, rsem = args2(q)
                second(axis, whole, 2, pair(relay2, q), pair(full2, q), ssem, rsem)
    for q in range(3):
        axis, whole, ssem, rsem = args2(q)
        third(axis, whole, pair(full2, q), ssem, rsem)
        first(ORDERS[q][0], piece(q, 2), 1, pair(relay1, q), sems(bs1, q), sems(br1, q))
    for q in range(3):
        second(
            ORDERS[q][0],
            lambda d: piece(q, d),
            1,
            pair(relay1, q),
            pair(full1, q),
            sems(bs1, q),
            sems(br1, q),
        )
    for q in range(3):
        ssem, rsem = sems(bs1, q), sems(br1, q)
        for kind, d in ((0, 1), (1, -1)):
            arrived(
                full1.at[q, kind], ssem[2 + kind], rsem[2 + kind], near[ORDERS[q][0], -d]
            )
        for s in range(2):
            value = piece(q, 0)[s].astype(jnp.float32)
            for kind in range(2):
                value = value + full1[q, kind, s].astype(jnp.float32)
            for h in range(2):
                base = h * 3072 + q * 1024 + s * 512
                columns = slice(base, base + 512)
                out_ref[:, columns] = (
                    hidden_ref[:, columns] + value[h * 8 : h * 8 + 8]
                ).astype(jnp.bfloat16)
    for copy in sent:
        copy.wait_send()


def experts(normed, hidden_state, routes, route_weight, gate_weight, up_weight, down_weight):
    piece = normed.reshape(8, 2, 3, 2, 512).transpose(2, 3, 1, 0, 4).reshape(3, 2, 16, 512)
    numbers = jnp.arange(16, dtype=jnp.int32)
    own = jnp.sum(
        jnp.where(routes[:, :, None] == numbers, route_weight[:, :, None], 0.0), axis=1
    )
    shares = lax.all_gather(own, ("ctx", "exp"), axis=0, tiled=True)
    mine = jnp.sum(jnp.where(numbers == lax.axis_index("exp"), shares, 0.0), axis=1)
    mine = mine.reshape(4, 2, 4, 2, 2, 8).transpose(0, 2, 3, 1, 4, 5).reshape(4, 4, 4, 2, 8)
    chosen = (mine > 0).astype(jnp.int32)
    slot = jnp.cumsum(chosen, axis=-1) - chosen + 4 * jnp.arange(2, dtype=jnp.int32)[:, None]
    letters = "zyx"
    picks = []
    for a1, a2, a3 in ORDERS:
        turn = [letters.index(a) for a in (a3, a2, a1)]
        t_slot = slot.transpose(*turn, 3, 4).reshape(4, 16, 2, 8)
        t_chosen = chosen.transpose(*turn, 3, 4).reshape(4, 16, 2, 8)
        chip = 8 * jnp.arange(16, dtype=jnp.int32)[:, None, None]
        target = jnp.where(t_chosen > 0, t_slot + chip, -1024).transpose(0, 2, 1, 3)
        sides = jnp.stack([target, target + 128], axis=3)
        picks.append(sides.reshape(4, 1, 512))
    pick = jnp.stack(picks)
    chip = 8 * jnp.arange(16, dtype=jnp.int32)[:, None, None]
    slots = jnp.where(chosen > 0, slot, -1024).reshape(4, 16, 2, 8) + chip
    slots = slots.transpose(0, 2, 1, 3).reshape(4, 256, 1)
    weights = mine.reshape(4, 16, 2, 8).transpose(0, 2, 1, 3).reshape(4, 256, 1)
    vmem = pl.BlockSpec(memory_space=pltpu.VMEM)
    hbm = pl.BlockSpec(memory_space=pl.ANY)
    dma = pltpu.SemaphoreType.DMA
    bf16 = jnp.bfloat16
    return pl.pallas_call(
        expert_kernel,
        name="experts",
        out_shape=jax.ShapeDtypeStruct((8, 6144), bf16),
        in_specs=[vmem] * 5 + [hbm] * 3,
        out_specs=vmem,
        scratch_shapes=[
            pltpu.VMEM((6144, 672), bf16),
            pltpu.VMEM((6144, 672), bf16),
            pltpu.VMEM((2, 672, 6144), bf16),
            pltpu.VMEM((2, 3, 4, 4, 4, 2, 16, 512), bf16),
            pltpu.VMEM((3, 4, 2, 2, 2, 16, 512), bf16),
            pltpu.VMEM((3, 4, 2, 4, 2, 16, 512), bf16),
            pltpu.VMEM((3, 2, 2, 2, 16, 512), bf16),
            pltpu.VMEM((3, 2, 4, 2, 16, 512), bf16),
            pltpu.VMEM((3, 2, 1, 16, 512), bf16),
            pltpu.VMEM((3, 2, 2, 16, 512), bf16),
            pltpu.VMEM((4, 4, 4, 8, 672), jnp.float32),
            pltpu.VMEM((4, 4, 4, 8, 672), jnp.float32),
            pltpu.VMEM((2, 4, 128, 672), bf16),
            pltpu.VMEM((4, 128, 672), bf16),
            dma((3,)),
            dma((3, 4)),
            dma((3, 4)),
            dma((3, 4)),
            dma((3, 4)),
            dma((3, 4, 4)),
            dma((3, 4, 4)),
            dma((3, 4, 4)),
            dma((3, 4, 4)),
            dma((2,)),
            dma((2,)),
            dma((3, 4, 4)),
            dma((3, 4, 4)),
            dma((3, 4)),
            dma((3, 4)),
            dma((3, 4)),
            dma((3, 4)),
        ],
        compiler_params=pltpu.CompilerParams(
            collective_id=1, has_side_effects=True, vmem_limit_bytes=63 * 1024 * 1024
        ),
    )(piece, hidden_state, pick, slots, weights, gate_weight, up_weight, down_weight)


def on_device(
    queries,
    keys_values,
    residual,
    out_weight,
    norm_gain,
    routes,
    route_weight,
    gate_weight,
    up_weight,
    down_weight,
):
    context_devices = lax.axis_size("ctx")
    expert_devices = lax.axis_size("exp")
    block_rows = queries.shape[0]
    local_heads = queries.shape[1] // HD
    token_rows = residual.shape[0]
    features = residual.shape[1]
    partner = from_partner(keys_values, "exp", 0)
    is_lower = lax.axis_index("exp") % 2 == 0
    joined = jnp.where(
        is_lower,
        jnp.concatenate([keys_values, partner], axis=2),
        jnp.concatenate([partner, keys_values], axis=2),
    )
    query_heads = queries.reshape(block_rows, local_heads, HD)
    first_position = lax.axis_index("ctx") * block_rows
    query_position = first_position + jnp.arange(block_rows, dtype=jnp.int32)
    last_position = first_position + block_rows - 1
    initial = (
        jnp.full((local_heads, block_rows), -jnp.inf, jnp.float32),
        jnp.zeros((local_heads, block_rows), jnp.float32),
        jnp.zeros((local_heads, block_rows, HD), jnp.float32),
    )
    portion = lax.all_gather(joined, "ctx", axis=1, tiled=True)

    def update(current):
        running_max, denominator, weighted_sum = current
        scores = jnp.einsum(
            "qhd,kd->hqk", query_heads, portion[0], preferred_element_type=jnp.float32
        ) / math.sqrt(HD)
        key_position = jnp.arange(portion.shape[1], dtype=jnp.int32)
        allowed = key_position[None, None, :] <= query_position[None, :, None]
        masked = jnp.where(allowed, scores, -jnp.inf)
        new_max = jnp.max(masked, axis=2)
        safe_max = jnp.where(new_max == -jnp.inf, 0.0, new_max)
        weights_now = jnp.where(allowed, jnp.exp(masked - safe_max[:, :, None]), 0.0)
        rescale = jnp.exp(running_max - safe_max)
        denominator = rescale * denominator + jnp.sum(weights_now, axis=2)
        weighted_sum = rescale[:, :, None] * weighted_sum + jnp.einsum(
            "hqk,kd->hqd",
            weights_now,
            portion[1].astype(jnp.float32),
            precision=lax.Precision.HIGHEST,
        )
        return (new_max, denominator, weighted_sum)

    running_max, denominator, weighted_sum = lax.cond(
        jnp.int32(0) > last_position, lambda unchanged: unchanged, update, initial
    )
    attended = (
        (weighted_sum / denominator[:, :, None])
        .transpose(1, 0, 2)
        .reshape(block_rows, local_heads * HD)
        .astype(jnp.bfloat16)
    )
    partial_value = jnp.dot(
        attended,
        lax.all_gather(out_weight, "ctx", axis=1, tiled=True),
        preferred_element_type=jnp.float32,
    )
    projected = lax.psum_scatter(
        partial_value.astype(jnp.bfloat16), "exp", scatter_dimension=0, tiled=True
    ).astype(jnp.float32)
    hidden_state = residual.astype(jnp.float32) + projected
    row_mean = jnp.mean(hidden_state, axis=1, keepdims=True)
    centered = hidden_state - row_mean
    variance = jnp.mean(centered * centered, axis=1, keepdims=True)
    normed = (centered * lax.rsqrt(variance + 1e-05) * norm_gain).astype(jnp.bfloat16)
    return experts(
        normed, hidden_state, routes, route_weight, gate_weight, up_weight, down_weight
    )


def solution(mesh):
    in_specs = (
        P("ctx", "exp"),
        P(None, "ctx", "exp"),
        P(("ctx", "exp"), None),
        P("exp", "ctx"),
        P(),
        P(("ctx", "exp"), None),
        P(("ctx", "exp"), None),
        P("exp", None, "ctx"),
        P("exp", None, "ctx"),
        P("exp", "ctx", None),
    )
    out_specs = P(("ctx", "exp"), None)
    return jax.shard_map(
        on_device, mesh=mesh, in_specs=in_specs, out_specs=out_specs, check_vma=False
    )
```

```python
import math

import jax
import jax.numpy as jnp
from jax import lax
from jax.experimental import pallas as pl
from jax.experimental.pallas import tpu as pltpu
from jax.sharding import PartitionSpec as P

HD = 128
MESH = pl.DeviceIdType.MESH
ORDERS = (("x", "y", "z"), ("y", "z", "x"), ("z", "x", "y"))
OFFSETS = (0, -1, 1, 2)
GROUPS_BACK = (2, 1, -1, 0)


def place():
    ctx = lax.axis_index("ctx")
    exp = lax.axis_index("exp")
    return {
        "z": ctx // 2,
        "x": ((exp // 2) % 2) * 2 + ctx % 2,
        "y": exp // 4,
        "k": exp % 2,
    }


def device_at(at):
    return (at["z"] * 2 + at["x"] % 2, at["y"] * 4 + (at["x"] // 2) * 2 + at["k"])


def moved(at, axis, by):
    there = dict(at)
    if axis == "k":
        there["k"] = 1 - at["k"]
    else:
        there[axis] = (at[axis] + by + 4) % 4
    return there


def send(source, target, send_sem, recv_sem, device):
    copy = pltpu.make_async_remote_copy(
        src_ref=source,
        dst_ref=target,
        send_sem=send_sem,
        recv_sem=recv_sem,
        device_id=device,
        device_id_type=MESH,
    )
    copy.start()
    return copy


def arrived(target, send_sem, recv_sem, device):
    pltpu.make_async_remote_copy(
        src_ref=target,
        dst_ref=target,
        send_sem=send_sem,
        recv_sem=recv_sem,
        device_id=device,
        device_id_type=MESH,
    ).wait_recv()


def expert_kernel(
    piece_ref,
    hidden_ref,
    table_ref,
    gate_hbm,
    up_hbm,
    down_hbm,
    out_ref,
    gate,
    up,
    down,
    rows,
    relay3,
    full3,
    relay2,
    full2,
    relay1,
    full1,
    gate_sum,
    up_sum,
    mixed,
    mixed_other,
    load_sem,
    s1,
    r1,
    s2,
    r2,
    s3,
    r3,
    sp,
    rp,
    sd,
    rd,
    bs3,
    br3,
    bs2,
    br2,
    bs1,
    br1,
):
    at = place()
    k = at["k"]
    near = {(a, d): device_at(moved(at, a, d)) for a in "xyz" for d in (1, -1)}
    partner = device_at(moved(at, "k", 1))

    barrier = pltpu.get_barrier_semaphore()
    for device in [*near.values(), partner]:
        pl.semaphore_signal(barrier, inc=1, device_id=device, device_id_type=MESH)
    pl.semaphore_wait(barrier, 7)

    def ring(axis, by):
        return (at[axis] + by + 4) % 4

    def piece(q, d):
        a1, a2, a3 = ORDERS[q]
        return rows.at[k, q, at[a3], at[a2], ring(a1, d)]

    def line(q, d):
        a1, a2, a3 = ORDERS[q]
        return rows.at[k, q, at[a3], ring(a2, d)]

    def group(q, d, g):
        a1, a2, a3 = ORDERS[q]
        return rows.at[k, q, ring(a3, d), ring(a2, g)]

    def group_other(q, d, g):
        a1, a2, a3 = ORDERS[q]
        return rows.at[1 - k, q, ring(a3, d), ring(a2, g)]

    sent = []

    def go(*args):
        sent.append(send(*args))

    for q in range(3):
        a1 = ORDERS[q][0]
        piece(q, 0)[...] = piece_ref[q]
        for kind, d in ((0, 1), (1, -1)):
            go(piece(q, 0), piece(q, 0), s1.at[q, kind], r1.at[q, kind], near[a1, d])

    loads = [
        pltpu.make_async_copy(gate_hbm.at[0], gate, load_sem.at[0]),
        pltpu.make_async_copy(up_hbm.at[0], up, load_sem.at[1]),
        pltpu.make_async_copy(down_hbm.at[0], down.at[0], load_sem.at[2]),
    ]
    for load in loads:
        load.start()
    go(down_hbm.at[0], down.at[1], sd.at[0], rd.at[0], partner)
    gate_sum[...] = jnp.zeros_like(gate_sum)
    up_sum[...] = jnp.zeros_like(up_sum)

    def half(ref, index, width):
        return ref.at[pl.ds(index * width, width)]

    def relay(q, axis, whole, kind, width, ssem, rsem):
        d = 1 if kind == 0 else -1
        arrived(whole(-d), ssem[kind], rsem[kind], near[axis, -d])
        part = half(whole(-d), kind, width)
        go(part, part, ssem[2 + kind], rsem[2 + kind], near[axis, d])

    def finish(q, axis, whole, width, ssem, rsem):
        for kind in (0, 1):
            d = 1 if kind == 0 else -1
            arrived(half(whole(2), kind, width), ssem[2 + kind], rsem[2 + kind], near[axis, -d])

    def sems(ref, *index):
        return [ref.at[(*index, kind)] for kind in range(4)]

    def to_ring(axis, whole, ssem, rsem):
        for kind, d in ((0, 1), (1, -1)):
            go(whole(0), whole(0), ssem[kind], rsem[kind], near[axis, d])

    def forward(q, d, g):
        go(group(q, d, g), group(q, d, g), sp.at[q, d % 4, g % 4], rp.at[q, d % 4, g % 4], partner)

    def one_plane(q, g):
        a3 = ORDERS[q][2]
        return a3, (lambda d: group(q, d, g)), sems(s3, q, g % 4), sems(r3, q, g % 4)

    for kind in (0, 1):
        for q in range(3):
            relay(q, ORDERS[q][0], lambda d: piece(q, d), kind, 1, sems(s1, q), sems(r1, q))
    for q in range(3):
        a1, a2, a3 = ORDERS[q]
        finish(q, a1, lambda d: piece(q, d), 1, sems(s1, q), sems(r1, q))
        to_ring(a2, lambda d: line(q, d), sems(s2, q), sems(r2, q))
        to_ring(*one_plane(q, 0))
        forward(q, 0, 0)
    for kind in (0, 1):
        g = -1 if kind == 0 else 1
        for q in range(3):
            a1, a2, a3 = ORDERS[q]
            relay(q, a2, lambda d: line(q, d), kind, 2, sems(s2, q), sems(r2, q))
            to_ring(*one_plane(q, g))
            forward(q, 0, g)
    for q in range(3):
        a1, a2, a3 = ORDERS[q]
        finish(q, a2, lambda d: line(q, d), 2, sems(s2, q), sems(r2, q))
        to_ring(*one_plane(q, 2))
        forward(q, 0, 2)

    def index_of(q, i3, i2):
        a1, a2, a3 = ORDERS[q]
        where = {a3: i3, a2: i2, a1: slice(None)}
        return where["z"], where["y"], where["x"]

    def table_rows(q, i3):
        row = lax.broadcasted_iota(jnp.int32, (32, 128), 0)
        a1, a2, a3 = ORDERS[q]
        spot = {a3: i3, a2: row // 4 % 4, a1: row % 4}
        source = (
            row // 16 * 64
            + spot["z"] * 16
            + spot["x"] % 2 * 8
            + spot["y"] * 2
            + spot["x"] // 2
        )
        wanted = source == lax.broadcasted_iota(jnp.int32, (32, 128), 1)
        chooser = jnp.where(wanted, 1.0, 0.0).astype(jnp.bfloat16)
        high = table_ref[...].astype(jnp.bfloat16)
        low = (table_ref[...] - high.astype(jnp.float32)).astype(jnp.bfloat16)
        return jnp.dot(chooser, high, preferred_element_type=jnp.float32) + jnp.dot(
            chooser, low, preferred_element_type=jnp.float32
        )

    def pick_targets(q, i3):
        codes = table_rows(q, i3)[:, :8].astype(jnp.bfloat16)
        tile = lax.broadcasted_iota(jnp.int32, (8, 512), 1) % 8
        repeat = jnp.where(tile == lax.broadcasted_iota(jnp.int32, (8, 512), 0), 1.0, 0.0)
        spread = jnp.dot(codes, repeat.astype(jnp.bfloat16), preferred_element_type=jnp.float32)
        column = lax.broadcasted_iota(jnp.int32, (32, 512), 1)
        own = column // 16 == lax.broadcasted_iota(jnp.int32, (32, 512), 0)
        code = jnp.sum(jnp.where(own, spread, 0.0), axis=0, keepdims=True)
        column = lax.broadcasted_iota(jnp.int32, (1, 512), 1)
        base = column // 8 % 2 * 128 + column // 16 % 16 * 8 + column // 256 * 4 - 1
        return jnp.where(code > 0, base.astype(jnp.float32) + code, -1.0)

    def slot_columns(z):
        found = table_rows(0, z)
        row = lax.broadcasted_iota(jnp.int32, (256, 32), 0)
        repeat = jnp.where(row // 8 == lax.broadcasted_iota(jnp.int32, (256, 32), 1), 1.0, 0.0)
        repeat = repeat.astype(jnp.bfloat16)
        high = found.astype(jnp.bfloat16)
        low = (found - high.astype(jnp.float32)).astype(jnp.bfloat16)
        spread = jnp.dot(repeat, high, preferred_element_type=jnp.float32) + jnp.dot(
            repeat, low, preferred_element_type=jnp.float32
        )
        lane = lax.broadcasted_iota(jnp.int32, (256, 128), 1)
        row = lax.broadcasted_iota(jnp.int32, (256, 128), 0)
        code = jnp.sum(jnp.where(lane == row % 8, spread, 0.0), axis=1, keepdims=True)
        share = jnp.sum(jnp.where(lane == row % 8 + 8, spread, 0.0), axis=1, keepdims=True)
        row = lax.broadcasted_iota(jnp.int32, (256, 1), 0)
        base = row // 8 % 16 * 8 + row // 128 * 4 - 1
        return jnp.where(code > 0, base.astype(jnp.float32) + code, -1.0), share

    def hidden_unit(q, d):
        a1, a2, a3 = ORDERS[q]
        for g in OFFSETS:
            arrived(
                group_other(q, d, g), sp.at[q, d % 4, g % 4], rp.at[q, d % 4, g % 4], partner
            )
        i3 = ring(a3, d)
        number = lax.broadcasted_iota(jnp.int32, (256, 512), 0).astype(jnp.float32)
        picker = jnp.where(number == pick_targets(q, i3), 1.0, 0.0).astype(jnp.bfloat16)
        picked = []
        for s in range(2):
            both = jnp.concatenate(
                [rows[c, q, i3, :, :, s].reshape(256, 512) for c in range(2)], axis=0
            )
            picked.append(
                jnp.dot(picker, both, preferred_element_type=jnp.float32).astype(jnp.bfloat16)
            )
        for weight, total in ((gate, gate_sum), (up, up_sum)):
            value = None
            for h in range(2):
                x = jnp.concatenate([p[h * 128 : h * 128 + 128] for p in picked], axis=1)
                base = h * 3072 + q * 1024
                term = lax.dot_general(
                    x,
                    weight[:, base : base + 1024],
                    (((1,), (1,)), ((), ())),
                    preferred_element_type=jnp.float32,
                )
                value = term if value is None else value + term
            for i2 in range(4):
                where = index_of(q, i3, i2)
                total[where] += value[i2 * 32 : i2 * 32 + 32].reshape(4, 8, 672)

    for t, g in enumerate(OFFSETS):
        for q in range(3):
            a3, whole, ssem, rsem = one_plane(q, g)
            for kind in (0, 1):
                relay(q, a3, whole, kind, 2, ssem, rsem)
                forward(q, -1 if kind == 0 else 1, g)
        if t == 0:
            loads[0].wait()
            loads[1].wait()
        if t >= 1:
            hidden_unit(t - 1, 0)
    for t, g in enumerate(OFFSETS):
        for q in range(3):
            a3, whole, ssem, rsem = one_plane(q, g)
            finish(q, a3, whole, 2, ssem, rsem)
            forward(q, 2, g)
        if t == 0:
            for q in range(3):
                hidden_unit(q, -1)
        if t == 1:
            for q in range(3):
                hidden_unit(q, 1)
    for q in range(3):
        hidden_unit(q, 2)

    number = lax.broadcasted_iota(jnp.int32, (256, 128), 1).astype(jnp.float32)
    for z in range(4):
        g = gate_sum[z].reshape(128, 672)
        u = up_sum[z].reshape(128, 672)
        activated = (g / (1.0 + jnp.exp(-g)) * u).astype(jnp.bfloat16)
        place_of, share = slot_columns(z)
        spread = jnp.where(number == place_of, 1.0, 0.0).astype(jnp.bfloat16)
        value = jnp.dot(spread, activated, preferred_element_type=jnp.float32) * share
        mixed[0, z] = value[:128].astype(jnp.bfloat16)
        mixed[1, z] = value[128:].astype(jnp.bfloat16)
    go(mixed.at[1 - k], mixed_other, sd.at[1], rd.at[1], partner)
    gate_sum[...] = mixed[k].astype(jnp.float32).reshape(4, 4, 4, 8, 672)
    loads[2].wait()
    arrived(down.at[1], sd.at[0], rd.at[0], partner)
    arrived(mixed_other, sd.at[1], rd.at[1], partner)
    up_sum[...] = mixed_other[...].astype(jnp.float32).reshape(4, 4, 4, 8, 672)
    for copy in sent:
        copy.wait_send()
    sent.clear()

    def down_unit(q, d):
        i3 = ring(ORDERS[q][2], d)
        a = [
            jnp.concatenate(
                [total[index_of(q, i3, i2)].reshape(32, 672) for i2 in range(4)], axis=0
            ).astype(jnp.bfloat16)
            for total in (gate_sum, up_sum)
        ]
        for s in range(2):
            sides = []
            for h in range(2):
                base = h * 3072 + q * 1024 + s * 512
                value = jnp.dot(
                    a[0], down[0, :, base : base + 512], preferred_element_type=jnp.float32
                ) + jnp.dot(
                    a[1], down[1, :, base : base + 512], preferred_element_type=jnp.float32
                )
                sides.append(value.reshape(16, 8, 512))
            joined = jnp.concatenate(sides, axis=1).astype(jnp.bfloat16)
            rows[k, q, i3, :, :, s] = joined.reshape(4, 4, 16, 512)

    def add_into(ref, *others):
        value = ref[...].astype(jnp.float32)
        for other in others:
            value = value + other[...].astype(jnp.float32)
        ref[...] = value.astype(jnp.bfloat16)

    def first(axis, far, width, slots, ssem, rsem):
        for kind, d in ((0, 1), (1, -1)):
            go(half(far, kind, width), slots[kind], ssem[kind], rsem[kind], near[axis, d])

    def second(axis, whole, width, slots, full, ssem, rsem):
        for kind, d in ((0, 1), (1, -1)):
            arrived(slots[kind], ssem[kind], rsem[kind], near[axis, -d])
            add_into(half(whole(d), kind, width), slots[kind])
            go(whole(d), full[kind], ssem[2 + kind], rsem[2 + kind], near[axis, d])

    def third(axis, whole, full, ssem, rsem):
        for kind, d in ((0, 1), (1, -1)):
            arrived(full[kind], ssem[2 + kind], rsem[2 + kind], near[axis, -d])
        add_into(whole(0), *full)

    def pair(ref, *index):
        return [ref.at[(*index, kind)] for kind in range(2)]

    for q in range(3):
        down_unit(q, 2)
        for g in GROUPS_BACK:
            first(
                ORDERS[q][2],
                group(q, 2, g),
                2,
                pair(relay3, q, g % 4),
                sems(bs3, q, g % 4),
                sems(br3, q, g % 4),
            )
    for q in range(3):
        down_unit(q, 1)
        down_unit(q, -1)
        for g in GROUPS_BACK:
            second(
                ORDERS[q][2],
                lambda d: group(q, d, g),
                2,
                pair(relay3, q, g % 4),
                pair(full3, q, g % 4),
                sems(bs3, q, g % 4),
                sems(br3, q, g % 4),
            )
    for q in range(3):
        down_unit(q, 0)

    def args2(q):
        return ORDERS[q][1], (lambda d: line(q, d)), sems(bs2, q), sems(br2, q)

    for g in GROUPS_BACK:
        for q in range(3):
            third(
                ORDERS[q][2],
                lambda d: group(q, d, g),
                pair(full3, q, g % 4),
                sems(bs3, q, g % 4),
                sems(br3, q, g % 4),
            )
            if g == 2:
                first(
                    ORDERS[q][1], line(q, 2), 2, pair(relay2, q), sems(bs2, q), sems(br2, q)
                )
        if g == -1:
            for q in range(3):
                axis, whole, ssem, rsem = args2(q)
                second(axis, whole, 2, pair(relay2, q), pair(full2, q), ssem, rsem)
    for q in range(3):
        axis, whole, ssem, rsem = args2(q)
        third(axis, whole, pair(full2, q), ssem, rsem)
        first(ORDERS[q][0], piece(q, 2), 1, pair(relay1, q), sems(bs1, q), sems(br1, q))
    for q in range(3):
        second(
            ORDERS[q][0],
            lambda d: piece(q, d),
            1,
            pair(relay1, q),
            pair(full1, q),
            sems(bs1, q),
            sems(br1, q),
        )
    for q in range(3):
        ssem, rsem = sems(bs1, q), sems(br1, q)
        for kind, d in ((0, 1), (1, -1)):
            arrived(
                full1.at[q, kind], ssem[2 + kind], rsem[2 + kind], near[ORDERS[q][0], -d]
            )
        for s in range(2):
            value = piece(q, 0)[s].astype(jnp.float32)
            for kind in range(2):
                value = value + full1[q, kind, s].astype(jnp.float32)
            for h in range(2):
                base = h * 3072 + q * 1024 + s * 512
                columns = slice(base, base + 512)
                out_ref[:, columns] = (
                    hidden_ref[:, columns] + value[h * 8 : h * 8 + 8]
                ).astype(jnp.bfloat16)
    for copy in sent:
        copy.wait_send()


def experts(piece, hidden_state, table, gate_weight, up_weight, down_weight):
    vmem = pl.BlockSpec(memory_space=pltpu.VMEM)
    hbm = pl.BlockSpec(memory_space=pl.ANY)
    dma = pltpu.SemaphoreType.DMA
    bf16 = jnp.bfloat16
    return pl.pallas_call(
        expert_kernel,
        name="experts",
        out_shape=jax.ShapeDtypeStruct((8, 6144), bf16),
        in_specs=[vmem] * 3 + [hbm] * 3,
        out_specs=vmem,
        scratch_shapes=[
            pltpu.VMEM((672, 6144), bf16),
            pltpu.VMEM((672, 6144), bf16),
            pltpu.VMEM((2, 672, 6144), bf16),
            pltpu.VMEM((2, 3, 4, 4, 4, 2, 16, 512), bf16),
            pltpu.VMEM((3, 4, 2, 2, 2, 16, 512), bf16),
            pltpu.VMEM((3, 4, 2, 4, 2, 16, 512), bf16),
            pltpu.VMEM((3, 2, 2, 2, 16, 512), bf16),
            pltpu.VMEM((3, 2, 4, 2, 16, 512), bf16),
            pltpu.VMEM((3, 2, 1, 16, 512), bf16),
            pltpu.VMEM((3, 2, 2, 16, 512), bf16),
            pltpu.VMEM((4, 4, 4, 8, 672), jnp.float32),
            pltpu.VMEM((4, 4, 4, 8, 672), jnp.float32),
            pltpu.VMEM((2, 4, 128, 672), bf16),
            pltpu.VMEM((4, 128, 672), bf16),
            dma((3,)),
            dma((3, 4)),
            dma((3, 4)),
            dma((3, 4)),
            dma((3, 4)),
            dma((3, 4, 4)),
            dma((3, 4, 4)),
            dma((3, 4, 4)),
            dma((3, 4, 4)),
            dma((2,)),
            dma((2,)),
            dma((3, 4, 4)),
            dma((3, 4, 4)),
            dma((3, 4)),
            dma((3, 4)),
            dma((3, 4)),
            dma((3, 4)),
        ],
        compiler_params=pltpu.CompilerParams(
            collective_id=1, has_side_effects=True, vmem_limit_bytes=63 * 1024 * 1024
        ),
    )(
        piece,
        hidden_state,
        table.reshape(128, 128),
        gate_weight.swapaxes(1, 2),
        up_weight.swapaxes(1, 2),
        down_weight,
    )


def fetch(source, target, send_sem, recv_sem, device):
    return pltpu.make_async_remote_copy(
        src_ref=source,
        dst_ref=target,
        send_sem=send_sem,
        recv_sem=recv_sem,
        device_id=device,
        device_id_type=MESH,
    )


def front_kernel(
    query_ref,
    kv_ref,
    residual_ref,
    gain_ref,
    routes_ref,
    share_ref,
    weight_hbm,
    piece_ref,
    hidden_ref,
    table_ref,
    blocks,
    scores,
    total,
    attended,
    gathered,
    weight,
    partial,
    partial_in,
    summed,
    summed_in,
    table,
    table1,
    table2,
    kv_s,
    kv_r,
    pair_s,
    pair_r,
    w_s,
    w_r,
    w_load,
    att_s,
    att_r,
    sum_s,
    sum_r,
    back_s,
    back_r,
    t1_s,
    t1_r,
    t2_s,
    t2_r,
    t3_s,
    t3_r,
):
    c = lax.axis_index("ctx")
    e = lax.axis_index("exp")
    k = e % 2
    p = e // 2
    other = 2 * p + 1 - k
    partner = (c, other)

    def along(j):
        return ((c + j) % 8, e)

    def along_other(j):
        return ((c + j) % 8, other)

    def across(i):
        return (c, 2 * ((p + i) % 8) + k)

    barrier = pltpu.get_barrier_semaphore()
    peers = [along(j) for j in range(1, 8)] + [along_other(j) for j in range(8)]
    peers += [across(i) for i in range(1, 8)]
    for device in peers:
        pl.semaphore_signal(barrier, inc=1, device_id=device, device_id_type=MESH)
    pl.semaphore_wait(barrier, len(peers))

    sent = []

    def go(*args):
        copy = fetch(*args)
        copy.start()
        sent.append(copy)

    blocks[c, k] = kv_ref[...]
    for j in range(1, 8):

        @pl.when(c + j < 8)
        def _(j=j):
            fetch(blocks.at[c, k], blocks.at[c, k], kv_s.at[j], kv_r.at[j], along(j)).start()

    go(blocks.at[c, k], blocks.at[c, k], pair_s.at[0], pair_r.at[0], partner)
    load = pltpu.make_async_copy(weight_hbm, weight.at[k], w_load)
    load.start()
    go(weight_hbm, weight.at[k], w_s, w_r, partner)

    expert = lax.broadcasted_iota(jnp.int32, (16, 8), 0)
    chosen = jnp.zeros((16, 8), jnp.float32)
    share = jnp.zeros((16, 8), jnp.float32)
    for t in range(4):
        hit = jnp.where(routes_ref[t : t + 1, :] == expert, 1.0, 0.0)
        chosen = chosen + hit
        share = share + hit * share_ref[t : t + 1, :]
    upto = jnp.where(
        lax.broadcasted_iota(jnp.int32, (8, 8), 0) <= lax.broadcasted_iota(jnp.int32, (8, 8), 1),
        1.0,
        0.0,
    )
    code = chosen * jnp.dot(chosen, upto, preferred_element_type=jnp.float32)
    filled = jnp.concatenate([code, share, jnp.zeros((16, 112), jnp.float32)], axis=1)
    for i in range(16):
        table[i % 2, i // 2] = filled[i : i + 1]
    table1[:, p] = table[:, p]
    for i in range(1, 8):
        there = (p + i) % 8
        go(table.at[:, there], table1.at[:, p], t1_s.at[i], t1_r.at[i], across(i))

    number = lax.broadcasted_iota(jnp.int32, (128, 128), 0)
    position = (number // 8 % 8) * 16 + (number // 64) * 8 + number % 8
    column = lax.broadcasted_iota(jnp.int32, (128, 128), 1)
    reorder = jnp.where(position == column, 1.0, 0.0).astype(jnp.bfloat16)
    turned = jnp.dot(reorder, query_ref[...], preferred_element_type=jnp.float32)
    query = jnp.concatenate([turned[:, h * 128 : h * 128 + 128] for h in range(3)], axis=0)
    query = query.astype(jnp.bfloat16)

    for j in range(1, 8):

        @pl.when(c - j >= 0)
        def _(j=j):
            region = blocks.at[c - j, k]
            fetch(region, region, kv_s.at[j], kv_r.at[j], along(8 - j)).wait_recv()
            fetch(region, region, pair_s.at[j], pair_r.at[j], partner).start()

    for i in range(1, 8):
        region = table1.at[:, (p - i + 8) % 8]
        fetch(region, region, t1_s.at[i], t1_r.at[i], across(8 - i)).wait_recv()
    table2[:, c] = table1[...]
    for j in range(1, 8):
        go(table1, table2.at[:, c], t2_s.at[j], t2_r.at[j], along(j))

    for j in range(8):
        columns = slice(j * 128, j * 128 + 128)

        @pl.when(c - j >= 0)
        def _(j=j, columns=columns):
            region = blocks.at[c - j, 1 - k]
            fetch(region, region, pair_s.at[j], pair_r.at[j], partner).wait_recv()
            keys = jnp.concatenate([blocks[c - j, half, 0] for half in range(2)], axis=0)
            score = jnp.dot(query, keys, preferred_element_type=jnp.float32) / math.sqrt(HD)
            if j == 0:
                allowed = jnp.concatenate([column <= position] * 3, axis=0)
                score = jnp.where(allowed, score, -1e30)
            scores[:, columns] = score

        @pl.when(c - j < 0)
        def _(columns=columns):
            scores[:, columns] = jnp.full((384, 128), -1e30, jnp.float32)

    highest = jnp.max(scores[...], axis=1, keepdims=True)
    total[...] = jnp.zeros_like(total)
    for j in range(8):

        @pl.when(c - j >= 0)
        def _(j=j):
            now = jnp.exp(scores[:, j * 128 : j * 128 + 128] - highest)
            values = jnp.concatenate([blocks[c - j, half, 1] for half in range(2)], axis=0)
            total[:, :128] += lax.dot_general(
                now.astype(jnp.bfloat16),
                values,
                (((1,), (1,)), ((), ())),
                preferred_element_type=jnp.float32,
            )
            total[:, 128:] += now

    bottom = jnp.sum(total[:, 128:], axis=1, keepdims=True)
    result = (total[:, :128] / bottom).astype(jnp.bfloat16)
    for h in range(3):
        for side in range(2):
            start = h * 128 + side * 64
            attended[side, :, h * 128 : h * 128 + 128] = result[start : start + 64]
    local = pltpu.make_async_copy(attended.at[k], gathered.at[c, k], att_r.at[0, 0])
    local.start()
    for j in range(8):
        if j > 0:
            go(attended.at[k], gathered.at[c, k], att_s.at[j, 0], att_r.at[j, 0], along(j))
        go(attended.at[1 - k], gathered.at[c, k], att_s.at[j, 1], att_r.at[j, 1], along_other(j))

    for j in range(1, 8):
        region = table2.at[:, (c - j + 8) % 8]
        fetch(region, region, t2_s.at[j], t2_r.at[j], along(8 - j)).wait_recv()
    table_ref[k] = table2[k]
    go(table2.at[1 - k], table_ref.at[k], t3_s, t3_r, partner)

    load.wait()
    fetch(weight.at[1 - k], weight.at[1 - k], w_s, w_r, partner).wait_recv()
    for part in range(2):
        for b in range(part * 4, part * 4 + 4):
            j = (c - b + 8) % 8
            region = gathered.at[b, k]
            fetch(region, region, att_s.at[j, 0], att_r.at[j, 0], partner).wait_recv()
            region = gathered.at[b, 1 - k]
            fetch(region, region, att_s.at[j, 1], att_r.at[j, 1], partner).wait_recv()
        value = None
        for side in range(2):
            term = jnp.dot(
                gathered[part * 4 : part * 4 + 4, side].reshape(256, 384),
                weight[side],
                preferred_element_type=jnp.float32,
            )
            value = term if value is None else value + term
        for i in range(8):
            partial[i, part] = jnp.concatenate(
                [value[b * 64 + i * 8 : b * 64 + i * 8 + 8] for b in range(4)], axis=0
            ).astype(jnp.bfloat16)
        for i in range(1, 8):
            go(
                partial.at[(p + i) % 8, part],
                partial_in.at[i, part],
                sum_s.at[i, part],
                sum_r.at[i, part],
                across(i),
            )
    for part in range(2):
        value = partial[p, part].astype(jnp.float32)
        for i in range(1, 8):
            region = partial_in.at[i, part]
            fetch(region, region, sum_s.at[i, part], sum_r.at[i, part], across(8 - i)).wait_recv()
            value = value + partial_in[i, part].astype(jnp.float32)
        summed[part * 4 : part * 4 + 4] = value.reshape(4, 8, 768)
    summed_in[c] = summed[c]
    for j in range(1, 8):
        go(summed.at[(c + j) % 8], summed_in.at[c], back_s.at[j], back_r.at[j], along(j))
    for j in range(1, 8):
        region = summed_in.at[(c - j + 8) % 8]
        fetch(region, region, back_s.at[j], back_r.at[j], along(8 - j)).wait_recv()
    for b in range(8):
        columns = slice(b * 768, b * 768 + 768)
        hidden_ref[:, columns] = residual_ref[:, columns].astype(jnp.float32) + summed_in[b]
    hidden = hidden_ref[...]
    centered = hidden - jnp.mean(hidden, axis=1, keepdims=True)
    variance = jnp.mean(centered * centered, axis=1, keepdims=True)
    normed = centered * lax.rsqrt(variance + 1e-05) * gain_ref[...]
    for q in range(3):
        for s in range(2):
            start = q * 1024 + s * 512
            piece_ref[q, s] = jnp.concatenate(
                [normed[:, start : start + 512], normed[:, 3072 + start : 3584 + start]], axis=0
            ).astype(jnp.bfloat16)

    fetch(table_ref.at[1 - k], table_ref.at[1 - k], t3_s, t3_r, partner).wait_recv()
    for copy in sent:
        copy.wait_send()
    for j in range(1, 8):

        @pl.when(c + j < 8)
        def _(j=j):
            region = blocks.at[c, k]
            fetch(region, region, kv_s.at[j], kv_r.at[j], along(j)).wait_send()

        @pl.when(c - j >= 0)
        def _(j=j):
            region = blocks.at[c - j, k]
            fetch(region, region, pair_s.at[j], pair_r.at[j], partner).wait_send()


def front(queries, keys_values, residual, out_weight, norm_gain, routes, route_weight):
    vmem = pl.BlockSpec(memory_space=pltpu.VMEM)
    dma = pltpu.SemaphoreType.DMA
    bf16 = jnp.bfloat16
    f32 = jnp.float32
    return pl.pallas_call(
        front_kernel,
        name="front",
        out_shape=(
            jax.ShapeDtypeStruct((3, 2, 16, 512), bf16),
            jax.ShapeDtypeStruct((8, 6144), f32),
            jax.ShapeDtypeStruct((2, 8, 8, 1, 128), f32),
        ),
        in_specs=[vmem] * 6 + [pl.BlockSpec(memory_space=pl.ANY)],
        out_specs=[vmem] * 3,
        scratch_shapes=[
            pltpu.VMEM((8, 2, 2, 64, 128), bf16),
            pltpu.VMEM((384, 1024), f32),
            pltpu.VMEM((384, 256), f32),
            pltpu.VMEM((2, 64, 384), bf16),
            pltpu.VMEM((8, 2, 64, 384), bf16),
            pltpu.VMEM((2, 384, 768), bf16),
            pltpu.VMEM((8, 2, 32, 768), bf16),
            pltpu.VMEM((8, 2, 32, 768), bf16),
            pltpu.VMEM((8, 8, 768), f32),
            pltpu.VMEM((8, 8, 768), f32),
            pltpu.VMEM((2, 8, 1, 128), f32),
            pltpu.VMEM((2, 8, 1, 128), f32),
            pltpu.VMEM((2, 8, 8, 1, 128), f32),
            dma((8,)),
            dma((8,)),
            dma((8,)),
            dma((8,)),
            dma,
            dma,
            dma,
            dma((8, 2)),
            dma((8, 2)),
            dma((8, 2)),
            dma((8, 2)),
            dma((8,)),
            dma((8,)),
            dma((8,)),
            dma((8,)),
            dma((8,)),
            dma((8,)),
            dma,
            dma,
        ],
        compiler_params=pltpu.CompilerParams(
            collective_id=2, has_side_effects=True, vmem_limit_bytes=40 * 1024 * 1024
        ),
    )(
        queries,
        keys_values.swapaxes(1, 2),
        residual,
        norm_gain.reshape(1, -1),
        routes.T,
        route_weight.T,
        out_weight,
    )


def on_device(
    queries,
    keys_values,
    residual,
    out_weight,
    norm_gain,
    routes,
    route_weight,
    gate_weight,
    up_weight,
    down_weight,
):
    piece, hidden_state, table = front(
        queries, keys_values, residual, out_weight, norm_gain, routes, route_weight
    )
    return experts(piece, hidden_state, table, gate_weight, up_weight, down_weight)


def solution(mesh):
    in_specs = (
        P("ctx", "exp"),
        P(None, "ctx", "exp"),
        P(("ctx", "exp"), None),
        P("exp", "ctx"),
        P(),
        P(("ctx", "exp"), None),
        P(("ctx", "exp"), None),
        P("exp", None, "ctx"),
        P("exp", None, "ctx"),
        P("exp", "ctx", None),
    )
    out_specs = P(("ctx", "exp"), None)
    return jax.shard_map(
        on_device, mesh=mesh, in_specs=in_specs, out_specs=out_specs, check_vma=False
    )
```

```python
import math
from types import SimpleNamespace

import jax
import jax.numpy as jnp
from jax import lax
from jax.experimental import pallas as pl
from jax.experimental.pallas import tpu as pltpu
from jax.sharding import PartitionSpec as P

HD = 128
MESH = pl.DeviceIdType.MESH
BF16 = jnp.bfloat16
F32 = jnp.float32
ORDERS = (("x", "y", "z"), ("y", "z", "x"), ("z", "x", "y"))
OFFSETS = (0, -1, 1, 2)
GROUPS_BACK = (2, 1, -1, 0)

SCRATCH = {
    "query": ((128, 384), BF16),
    "residual": ((8, 6144), BF16),
    "gain": ((1, 6144), F32),
    "routes": ((4, 8), jnp.int32),
    "share": ((4, 8), F32),
    "blocks": ((8, 2, 2, 64, 128), BF16),
    "attended": ((2, 64, 384), BF16),
    "partial_in": ((8, 2, 32, 768), BF16),
    "summed": ((8, 8, 768), F32),
    "summed_in": ((8, 8, 768), F32),
    "hidden": ((8, 6144), F32),
    "table": ((2, 8, 1, 128), F32),
    "table1": ((2, 8, 1, 128), F32),
    "table2": ((2, 8, 8, 1, 128), F32),
    "tables": ((2, 8, 8, 1, 128), F32),
    "targets": ((8, 1, 512), F32),
    "gate": ((672, 6144), BF16),
    "up": ((672, 6144), BF16),
    "down": ((2, 672, 6144), BF16),
    "rows": ((2, 3, 4, 4, 4, 2, 16, 512), BF16),
    "relay3": ((3, 2, 4, 2, 2, 16, 512), BF16),
    "full3": ((3, 2, 4, 2, 4, 16, 512), BF16),
    "full2": ((3, 2, 4, 4, 16, 512), BF16),
    "full1": ((3, 2, 4, 16, 512), BF16),
    "selected": ((512, 3072), BF16),
    "sums": ((512, 1536), F32),
    "mixed": ((2, 512, 672), BF16),
    "mixed_other": ((512, 672), BF16),
}
SEMAPHORES = {
    "load": (10,),
    "kv": (8,),
    "pair": (8,),
    "weight": (1,),
    "att": (8, 2),
    "sum": (8, 2),
    "back": (8,),
    "t1": (8,),
    "t2": (8,),
    "t3": (1,),
    "ag1": (3, 4),
    "ag2": (3, 4),
    "ag3": (3, 2, 4, 4),
    "fwd": (3, 2, 4, 4),
    "swap": (1,),
    "mix": (4,),
    "rs3": (3, 2, 4, 4),
    "rs2": (3, 2, 4),
    "rs1": (3, 2, 4),
}
INPUTS = (
    "query_hbm",
    "kv_hbm",
    "residual_hbm",
    "gain_hbm",
    "routes_hbm",
    "share_hbm",
    "weight_hbm",
    "gate_hbm",
    "up_hbm",
    "down_hbm",
)


def device_at(at):
    return (at["z"] * 2 + at["x"] % 2, at["y"] * 4 + (at["x"] // 2) * 2 + at["k"])


def moved(at, axis, by):
    there = dict(at)
    there[axis] = (at[axis] + by + 4) % 4
    return there


def column_of(h, s, q):
    return h * 3072 + s * 1536 + q * 512


class Links:
    def __init__(self, refs):
        self.refs = refs
        self.sent = []

    def copy(self, name, index, source, target, device):
        return pltpu.make_async_remote_copy(
            src_ref=source,
            dst_ref=target,
            send_sem=getattr(self.refs, name + "_s").at[index],
            recv_sem=getattr(self.refs, name + "_r").at[index],
            device_id=device,
            device_id_type=MESH,
        )

    def go(self, name, index, source, target, device):
        copy = self.copy(name, index, source, target, device)
        copy.start()
        self.sent.append(copy)

    def arrived(self, name, index, target, device):
        self.copy(name, index, target, target, device).wait_recv()

    def settle(self):
        for copy in self.sent:
            copy.wait_send()
        self.sent.clear()


def row_table(r, links, across, p):
    expert = lax.broadcasted_iota(jnp.int32, (16, 8), 0)
    chosen = jnp.zeros((16, 8), F32)
    share = jnp.zeros((16, 8), F32)
    for t in range(4):
        hit = jnp.where(r.routes[t : t + 1, :] == expert, 1.0, 0.0)
        chosen = chosen + hit
        share = share + hit * r.share[t : t + 1, :]
    upto = jnp.where(
        lax.broadcasted_iota(jnp.int32, (8, 8), 0) <= lax.broadcasted_iota(jnp.int32, (8, 8), 1),
        1.0,
        0.0,
    )
    code = chosen * jnp.dot(chosen, upto, preferred_element_type=F32)
    filled = jnp.concatenate([code, share, jnp.zeros((16, 112), F32)], axis=1)
    for i in range(16):
        r.table[i % 2, i // 2] = filled[i : i + 1]
    r.table1[:, p] = r.table[:, p]
    for i in range(1, 8):
        links.go("t1", i, r.table.at[:, (p + i) % 8], r.table1.at[:, p], across(i))


def layer_kernel(*refs):
    names = INPUTS + ("out",) + tuple(SCRATCH)
    for name in SEMAPHORES:
        names += (name + "_s", name + "_r")
    r = SimpleNamespace(**dict(zip(names, refs, strict=True)))
    links = Links(r)
    go, arrived = links.go, links.arrived

    c = lax.axis_index("ctx")
    e = lax.axis_index("exp")
    k = e % 2
    p = e // 2
    other = 2 * p + 1 - k
    partner = (c, other)
    at = {"z": c // 2, "x": (p % 2) * 2 + c % 2, "y": e // 4, "k": k}
    near = {(a, d): device_at(moved(at, a, d)) for a in "xyz" for d in (1, -1, 2, -2)}

    def along(j):
        return ((c + j) % 8, e)

    def along_other(j):
        return ((c + j) % 8, other)

    def across(i):
        return (c, 2 * ((p + i) % 8) + k)

    def load(i, source, target):
        copy = pltpu.make_async_copy(source, target, r.load_s.at[i])
        copy.start()
        return copy

    loads = [
        load(0, r.kv_hbm, r.blocks.at[c, k]),
        load(1, r.query_hbm, r.query),
        load(2, r.routes_hbm, r.routes),
        load(3, r.share_hbm, r.share),
        load(4, r.residual_hbm, r.residual),
        load(5, r.gain_hbm, r.gain),
    ]

    barrier = pltpu.get_barrier_semaphore()
    peers = [along(j) for j in range(1, 8)] + [along_other(j) for j in range(8)]
    peers += [across(i) for i in range(1, 8)] + [near["x", 1], near["x", -1]]
    for device in peers:
        pl.semaphore_signal(barrier, inc=1, device_id=device, device_id_type=MESH)
    pl.semaphore_wait(barrier, len(peers))

    loads[0].wait()
    own_block = r.blocks.at[c, k]
    go("pair", 0, own_block, own_block, partner)
    for j in range(1, 8):

        @pl.when(c + j < 8)
        def _(j=j):
            links.copy("kv", j, own_block, own_block, along(j)).start()

    def out_weight(side):
        return r.selected.at[pl.ds(0, 384), pl.ds(768 + side * 768, 768)]

    own_weight = load(6, r.weight_hbm, out_weight(k))
    go("weight", 0, r.weight_hbm, out_weight(k), partner)

    loads[2].wait()
    loads[3].wait()
    row_table(r, links, across, p)

    number = lax.broadcasted_iota(jnp.int32, (128, 128), 0)
    position = (number // 8 % 8) * 16 + (number // 64) * 8 + number % 8
    column = lax.broadcasted_iota(jnp.int32, (128, 128), 1)
    reorder = jnp.where(position == column, 1.0, 0.0).astype(BF16)
    loads[1].wait()
    turned = jnp.dot(reorder, r.query[...], preferred_element_type=F32)
    query = jnp.concatenate([turned[:, h * 128 : h * 128 + 128] for h in range(3)], axis=0)
    query = query.astype(BF16)

    for j in range(1, 8):

        @pl.when(c - j >= 0)
        def _(j=j):
            region = r.blocks.at[c - j, k]
            arrived("kv", j, region, along(8 - j))
            links.copy("pair", j, region, region, partner).start()

    big_loads = [
        load(7, r.gate_hbm.at[0], r.gate),
        load(8, r.up_hbm.at[0], r.up),
        load(9, r.down_hbm.at[0], r.down.at[0]),
    ]
    go("swap", 0, r.down_hbm.at[0], r.down.at[1], partner)

    for i in range(1, 8):
        arrived("t1", i, r.table1.at[:, (p - i + 8) % 8], across(8 - i))
    r.table2[:, c] = r.table1[...]
    for j in range(1, 8):
        go("t2", j, r.table1, r.table2.at[:, c], along(j))

    for j in range(8):
        columns = slice(j * 128, j * 128 + 128)

        @pl.when(c - j >= 0)
        def _(j=j, columns=columns):
            arrived("pair", j, r.blocks.at[c - j, 1 - k], partner)
            keys = jnp.concatenate([r.blocks[c - j, half, 0] for half in range(2)], axis=0)
            score = jnp.dot(query, keys, preferred_element_type=F32) / math.sqrt(HD)
            if j == 0:
                allowed = jnp.concatenate([column <= position] * 3, axis=0)
                score = jnp.where(allowed, score, -1e30)
            r.sums[0:384, columns] = score

        @pl.when(c - j < 0)
        def _(columns=columns):
            r.sums[0:384, columns] = jnp.full((384, 128), -1e30, F32)

    highest = jnp.max(r.sums[0:384, 0:1024], axis=1, keepdims=True)
    r.sums[0:384, 1024:1280] = jnp.zeros((384, 256), F32)
    for j in range(8):

        @pl.when(c - j >= 0)
        def _(j=j):
            now = jnp.exp(r.sums[0:384, j * 128 : j * 128 + 128] - highest)
            values = jnp.concatenate([r.blocks[c - j, half, 1] for half in range(2)], axis=0)
            r.sums[0:384, 1024:1152] += lax.dot_general(
                now.astype(BF16), values, (((1,), (1,)), ((), ())), preferred_element_type=F32
            )
            r.sums[0:384, 1152:1280] += now

    bottom = jnp.sum(r.sums[0:384, 1152:1280], axis=1, keepdims=True)
    result = (r.sums[0:384, 1024:1152] / bottom).astype(BF16)
    for h in range(3):
        for side in range(2):
            start = h * 128 + side * 64
            r.attended[side, :, h * 128 : h * 128 + 128] = result[start : start + 64]

    def gathered(b, side):
        return r.selected.at[pl.ds(b * 64, 64), pl.ds(pl.multiple_of(side * 384, 128), 384)]

    own_rows = pltpu.make_async_copy(r.attended.at[k], gathered(c, k), r.att_r.at[0, 0])
    own_rows.start()
    for j in range(8):
        if j > 0:
            go("att", (j, 0), r.attended.at[k], gathered(c, k), along(j))
        go("att", (j, 1), r.attended.at[1 - k], gathered(c, k), along_other(j))

    for j in range(1, 8):
        arrived("t2", j, r.table2.at[:, (c - j + 8) % 8], along(8 - j))
    r.tables[k] = r.table2[k]
    go("t3", 0, r.table2.at[1 - k], r.tables.at[k], partner)

    own_weight.wait()
    arrived("weight", 0, out_weight(1 - k), partner)

    def partial(i, part):
        return r.selected.at[pl.ds((i * 2 + part) * 32, 32), pl.ds(2304, 768)]

    for part in range(2):
        for b in range(part * 4, part * 4 + 4):
            j = (c - b + 8) % 8
            arrived("att", (j, 0), gathered(b, k), partner)
            arrived("att", (j, 1), gathered(b, 1 - k), partner)
        value = None
        for side in range(2):
            term = jnp.dot(
                r.selected[part * 256 : part * 256 + 256, side * 384 : side * 384 + 384],
                r.selected[0:384, 768 + side * 768 : 1536 + side * 768],
                preferred_element_type=F32,
            )
            value = term if value is None else value + term
        for i in range(8):
            partial(i, part)[...] = jnp.concatenate(
                [value[b * 64 + i * 8 : b * 64 + i * 8 + 8] for b in range(4)], axis=0
            ).astype(BF16)
        for i in range(1, 8):
            go("sum", (i, part), partial((p + i) % 8, part), r.partial_in.at[i, part], across(i))
    for part in range(2):
        value = partial(p, part)[...].astype(F32)
        for i in range(1, 8):
            arrived("sum", (i, part), r.partial_in.at[i, part], across(8 - i))
            value = value + r.partial_in[i, part].astype(F32)
        r.summed[part * 4 : part * 4 + 4] = value.reshape(4, 8, 768)
    r.summed_in[c] = r.summed[c]
    for j in range(1, 8):
        go("back", j, r.summed.at[(c + j) % 8], r.summed_in.at[c], along(j))
    for j in range(1, 8):
        arrived("back", j, r.summed_in.at[(c - j + 8) % 8], along(8 - j))
    for b in range(8):
        columns = slice(b * 768, b * 768 + 768)
        if b == 0:
            loads[4].wait()
            loads[5].wait()
        r.hidden[:, columns] = r.residual[:, columns].astype(F32) + r.summed_in[b]
    hidden = r.hidden[...]
    centered = hidden - jnp.mean(hidden, axis=1, keepdims=True)
    variance = jnp.mean(centered * centered, axis=1, keepdims=True)
    normed = centered * lax.rsqrt(variance + 1e-05) * r.gain[...]

    links.settle()

    def ring(axis, by):
        return (at[axis] + by + 4) % 4

    def piece(q, d):
        a1, a2, a3 = ORDERS[q]
        return r.rows.at[k, q, at[a3], at[a2], ring(a1, d)]

    def line(q, d):
        a1, a2, a3 = ORDERS[q]
        return r.rows.at[k, q, at[a3], ring(a2, d)]

    def group(q, s, d, g, side=None):
        a1, a2, a3 = ORDERS[q]
        side = k if side is None else side
        return r.rows.at[side, q, ring(a3, d), ring(a2, g), :, s]

    def half(ref, index):
        return ref.at[pl.ds(index * 2, 2)]

    for q in range(3):
        for s in range(2):
            low, high = column_of(0, s, q), column_of(1, s, q)
            piece(q, 0)[s] = jnp.concatenate(
                [normed[:, low : low + 512], normed[:, high : high + 512]], axis=0
            ).astype(BF16)
        for d in (1, -1, 2):
            go("ag1", (q, d % 4), piece(q, 0), piece(q, 0), near[ORDERS[q][0], d])

    arrived("t3", 0, r.tables.at[1 - k], partner)
    tables = r.tables[...].reshape(128, 128)
    table_high = tables.astype(BF16)
    table_low = (tables - table_high.astype(F32)).astype(BF16)

    def table_rows(turn, z):
        row = lax.broadcasted_iota(jnp.int32, (32, 128), 0)
        slow, fast = row // 4 % 4, row % 4
        x, y = (slow, fast) if turn else (fast, slow)
        source = row // 16 * 64 + z * 16 + x % 2 * 8 + y * 2 + x // 2
        wanted = source == lax.broadcasted_iota(jnp.int32, (32, 128), 1)
        chooser = jnp.where(wanted, 1.0, 0.0).astype(BF16)
        return jnp.dot(chooser, table_high, preferred_element_type=F32) + jnp.dot(
            chooser, table_low, preferred_element_type=F32
        )

    def pick_targets(turn, z):
        codes = table_rows(turn, z)[:, :8].astype(BF16)
        tile = lax.broadcasted_iota(jnp.int32, (8, 512), 1) % 8
        repeat = jnp.where(tile == lax.broadcasted_iota(jnp.int32, (8, 512), 0), 1.0, 0.0)
        spread = jnp.dot(codes, repeat.astype(BF16), preferred_element_type=F32)
        column = lax.broadcasted_iota(jnp.int32, (32, 512), 1)
        own = column // 16 == lax.broadcasted_iota(jnp.int32, (32, 512), 0)
        code = jnp.sum(jnp.where(own, spread, 0.0), axis=0, keepdims=True)
        column = lax.broadcasted_iota(jnp.int32, (1, 512), 1)
        chip = column // 16 % 16
        if turn:
            chip = chip % 4 * 4 + chip // 4
        base = column // 8 % 2 * 128 + chip * 8 + column // 256 * 4 - 1
        return jnp.where(code > 0, base.astype(F32) + code, -1.0)

    def slot_columns(z):
        found = table_rows(0, z)
        row = lax.broadcasted_iota(jnp.int32, (256, 32), 0)
        repeat = jnp.where(row // 8 == lax.broadcasted_iota(jnp.int32, (256, 32), 1), 1.0, 0.0)
        repeat = repeat.astype(BF16)
        high = found.astype(BF16)
        low = (found - high.astype(F32)).astype(BF16)
        spread = jnp.dot(repeat, high, preferred_element_type=F32) + jnp.dot(
            repeat, low, preferred_element_type=F32
        )
        lane = lax.broadcasted_iota(jnp.int32, (256, 128), 1)
        row = lax.broadcasted_iota(jnp.int32, (256, 128), 0)
        code = jnp.sum(jnp.where(lane == row % 8, spread, 0.0), axis=1, keepdims=True)
        share = jnp.sum(jnp.where(lane == row % 8 + 8, spread, 0.0), axis=1, keepdims=True)
        row = lax.broadcasted_iota(jnp.int32, (256, 1), 0)
        base = row // 8 % 16 * 8 + row // 128 * 4 - 1
        return jnp.where(code > 0, base.astype(F32) + code, -1.0), share

    def forward(q, s, d, g):
        region = group(q, s, d, g)
        go("fwd", (q, s, d % 4, g % 4), region, region, partner)

    def ring_send(q, s, g):
        for kind, d in ((0, 1), (1, -1)):
            region = group(q, s, 0, g)
            go("ag3", (q, s, g % 4, kind), region, region, near[ORDERS[q][2], d])

    def ring_relay(q, s, g):
        for kind, d in ((0, 1), (1, -1)):
            whole = group(q, s, -d, g)
            arrived("ag3", (q, s, g % 4, kind), whole, near[ORDERS[q][2], -d])
            part = half(whole, kind)
            go("ag3", (q, s, g % 4, 2 + kind), part, part, near[ORDERS[q][2], d])
            forward(q, s, -d, g)

    def ring_finish(q, s, g):
        for kind, d in ((0, 1), (1, -1)):
            part = half(group(q, s, 2, g), kind)
            arrived("ag3", (q, s, g % 4, 2 + kind), part, near[ORDERS[q][2], -d])
        forward(q, s, 2, g)

    for q in range(3):
        for d in (1, -1, 2):
            arrived("ag1", (q, d % 4), piece(q, -d), near[ORDERS[q][0], -d])
        for d in (1, -1, 2):
            go("ag2", (q, d % 4), line(q, 0), line(q, 0), near[ORDERS[q][1], d])
        ring_send(q, 0, 0)
        for s in range(2):
            forward(q, s, 0, 0)
    for z in range(4):
        for turn in range(2):
            r.targets[turn * 4 + z] = pick_targets(turn, z)
    for g in (-1, 1, 2):
        for q in range(3):
            arrived("ag2", (q, -g % 4), line(q, g), near[ORDERS[q][1], g])
            ring_send(q, 0, g)
            for s in range(2):
                forward(q, s, 0, g)
    for g in OFFSETS:
        for q in range(3):
            ring_relay(q, 0, g)
            ring_send(q, 1, g)
    for g in OFFSETS:
        for q in range(3):
            ring_finish(q, 0, g)

    def select(s):
        for q in range(3):
            for d in OFFSETS:
                for g in OFFSETS:
                    arrived(
                        "fwd", (q, s, d % 4, g % 4), group(q, s, d, g, 1 - k), partner
                    )
        slots = lax.broadcasted_iota(jnp.int32, (256, 512), 0).astype(F32)
        for z in range(4):
            for q in range(3):
                picker = jnp.where(slots == r.targets[(4 if q == 1 else 0) + z], 1.0, 0.0)
                sides = []
                for side in range(2):
                    found = (
                        r.rows[side, q, z, :, :, s],
                        r.rows[side, q, :, z, :, s],
                        r.rows[side, q, :, :, z, s],
                    )[q]
                    sides.append(found.reshape(256, 512))
                value = jnp.dot(
                    picker.astype(BF16),
                    jnp.concatenate(sides, axis=0),
                    preferred_element_type=F32,
                ).astype(BF16)
                for h in range(2):
                    start = h * 1536 + q * 512
                    r.selected[z * 128 : z * 128 + 128, start : start + 512] = value[
                        h * 128 : h * 128 + 128
                    ]

    def product(weight, s):
        value = None
        for h in range(2):
            start = column_of(h, s, 0)
            term = lax.dot_general(
                r.selected[:, h * 1536 : h * 1536 + 1536],
                weight[:, start : start + 1536],
                (((1,), (1,)), ((), ())),
                preferred_element_type=F32,
            )
            value = term if value is None else value + term
        return value

    select(0)
    for q in range(3):
        ring_relay(q, 1, 0)
    big_loads[0].wait()
    r.sums[:, 0:672] = product(r.gate, 0)
    for g in (-1, 1):
        for q in range(3):
            ring_relay(q, 1, g)
    big_loads[1].wait()
    r.sums[:, 768:1440] = product(r.up, 0)
    for q in range(3):
        ring_relay(q, 1, 2)
    for g in OFFSETS:
        for q in range(3):
            ring_finish(q, 1, g)
    select(1)
    r.sums[:, 0:672] += product(r.gate, 1)
    r.sums[:, 768:1440] += product(r.up, 1)

    number = lax.broadcasted_iota(jnp.int32, (256, 128), 1).astype(F32)
    for z in range(4):
        block = slice(z * 128, z * 128 + 128)
        g = r.sums[block, 0:672]
        u = r.sums[block, 768:1440]
        activated = (g / (1.0 + jnp.exp(-g)) * u).astype(BF16)
        place_of, share = slot_columns(z)
        spread = jnp.where(number == place_of, 1.0, 0.0).astype(BF16)
        value = jnp.dot(spread, activated, preferred_element_type=F32) * share
        r.mixed[0, block] = value[:128].astype(BF16)
        r.mixed[1, block] = value[128:].astype(BF16)
        go(
            "mix",
            z,
            r.mixed.at[1 - k, pl.ds(z * 128, 128)],
            r.mixed_other.at[pl.ds(z * 128, 128)],
            partner,
        )
    big_loads[2].wait()
    arrived("swap", 0, r.down.at[1], partner)
    for z in range(4):
        arrived("mix", z, r.mixed_other.at[pl.ds(z * 128, 128)], partner)
    links.settle()

    def down_unit(q, s):
        sides = []
        for h in range(2):
            start = column_of(h, s, q)
            value = jnp.dot(
                r.mixed[k], r.down[0, :, start : start + 512], preferred_element_type=F32
            ) + jnp.dot(
                r.mixed_other[...], r.down[1, :, start : start + 512], preferred_element_type=F32
            )
            sides.append(value.reshape(64, 8, 512))
        joined = jnp.concatenate(sides, axis=1).astype(BF16).reshape(4, 4, 4, 16, 512)
        if q == 0:
            r.rows[k, 0, :, :, :, s] = joined
        elif q == 1:
            for x in range(4):
                r.rows[k, 1, x, :, :, s] = joined[:, :, x]
        else:
            for y in range(4):
                for x in range(4):
                    r.rows[k, 2, y, x, :, s] = joined[:, y, x]

    def add_into(ref, *others):
        value = ref[...].astype(F32)
        for other_ref in others:
            value = value + other_ref[...].astype(F32)
        ref[...] = value.astype(BF16)

    def back_first(q, s):
        for g in GROUPS_BACK:
            for kind, d in ((0, 1), (1, -1)):
                go(
                    "rs3",
                    (q, s, g % 4, kind),
                    half(group(q, s, 2, g), kind),
                    r.relay3.at[q, s, g % 4, kind],
                    near[ORDERS[q][2], d],
                )

    def back_second(q, s):
        for g in GROUPS_BACK:
            for kind, d in ((0, 1), (1, -1)):
                slot = r.relay3.at[q, s, g % 4, kind]
                arrived("rs3", (q, s, g % 4, kind), slot, near[ORDERS[q][2], -d])
                whole = group(q, s, d, g)
                add_into(half(whole, kind), slot)
                go(
                    "rs3",
                    (q, s, g % 4, 2 + kind),
                    whole,
                    r.full3.at[q, s, g % 4, kind],
                    near[ORDERS[q][2], d],
                )

    def back_third(q, s, g):
        slots = [r.full3.at[q, s, g % 4, kind] for kind in range(2)]
        for kind, d in ((0, 1), (1, -1)):
            arrived("rs3", (q, s, g % 4, 2 + kind), slots[kind], near[ORDERS[q][2], -d])
        whole = group(q, s, 0, g)
        add_into(whole, *slots)
        if g != 0:
            go("rs2", (q, s, g % 4), whole, r.full2.at[q, s, g % 4], near[ORDERS[q][1], g])

    def back_line(q, s):
        slots = [r.full2.at[q, s, g % 4] for g in (1, -1, 2)]
        for g, slot in zip((1, -1, 2), slots, strict=True):
            arrived("rs2", (q, s, g % 4), slot, near[ORDERS[q][1], -g])
        add_into(group(q, s, 0, 0), *slots)
        for d in (1, -1, 2):
            go(
                "rs1",
                (q, s, d % 4),
                piece(q, d).at[s],
                r.full1.at[q, s, d % 4],
                near[ORDERS[q][0], d],
            )

    def back_end(q, s):
        value = piece(q, 0)[s].astype(F32)
        for d in (1, -1, 2):
            slot = r.full1.at[q, s, d % 4]
            arrived("rs1", (q, s, d % 4), slot, near[ORDERS[q][0], -d])
            value = value + slot[...].astype(F32)
        for h in range(2):
            start = column_of(h, s, q)
            columns = slice(start, start + 512)
            r.out[:, columns] = (r.hidden[:, columns] + value[h * 8 : h * 8 + 8]).astype(BF16)

    for q in range(3):
        down_unit(q, 0)
        back_first(q, 0)
    for q in range(3):
        down_unit(q, 1)
        back_first(q, 1)
        back_second(q, 0)
    for q in range(3):
        back_second(q, 1)
    for s in range(2):
        for g in GROUPS_BACK:
            for q in range(3):
                back_third(q, s, g)
    for s in range(2):
        for q in range(3):
            back_line(q, s)
    for s in range(2):
        for q in range(3):
            back_end(q, s)

    links.settle()
    for j in range(1, 8):

        @pl.when(c + j < 8)
        def _(j=j):
            links.copy("kv", j, own_block, own_block, along(j)).wait_send()

        @pl.when(c - j >= 0)
        def _(j=j):
            region = r.blocks.at[c - j, k]
            links.copy("pair", j, region, region, partner).wait_send()


def on_device(
    queries,
    keys_values,
    residual,
    out_weight,
    norm_gain,
    routes,
    route_weight,
    gate_weight,
    up_weight,
    down_weight,
):
    scratch = [pltpu.VMEM(shape, kind) for shape, kind in SCRATCH.values()]
    for shape in SEMAPHORES.values():
        scratch += [pltpu.SemaphoreType.DMA(shape)] * 2
    return pl.pallas_call(
        layer_kernel,
        name="layer",
        out_shape=jax.ShapeDtypeStruct(residual.shape, BF16),
        in_specs=[pl.BlockSpec(memory_space=pl.ANY)] * len(INPUTS),
        out_specs=pl.BlockSpec(memory_space=pltpu.VMEM),
        scratch_shapes=scratch,
        compiler_params=pltpu.CompilerParams(
            collective_id=1, has_side_effects=True, vmem_limit_bytes=64 * 1024 * 1024 - 65536
        ),
    )(
        queries,
        keys_values.swapaxes(1, 2),
        residual,
        norm_gain.reshape(1, -1),
        routes.T,
        route_weight.T,
        out_weight,
        gate_weight.swapaxes(1, 2),
        up_weight.swapaxes(1, 2),
        down_weight,
    )


def solution(mesh):
    in_specs = (
        P("ctx", "exp"),
        P(None, "ctx", "exp"),
        P(("ctx", "exp"), None),
        P("exp", "ctx"),
        P(),
        P(("ctx", "exp"), None),
        P(("ctx", "exp"), None),
        P("exp", None, "ctx"),
        P("exp", None, "ctx"),
        P("exp", "ctx", None),
    )
    out_specs = P(("ctx", "exp"), None)
    return jax.shard_map(
        on_device, mesh=mesh, in_specs=in_specs, out_specs=out_specs, check_vma=False
    )
```

```python
import math
from types import SimpleNamespace

import jax
import jax.numpy as jnp
from jax import lax
from jax.experimental import pallas as pl
from jax.experimental.pallas import tpu as pltpu
from jax.sharding import PartitionSpec as P

HD = 128
MESH = pl.DeviceIdType.MESH
BF16 = jnp.bfloat16
F32 = jnp.float32
ORDERS = (("x", "y", "z"), ("y", "z", "x"), ("z", "x", "y"))
OFFSETS = (0, -1, 1, 2)
GROUPS_BACK = (2, 1, -1, 0)

SCRATCH = {
    "query": ((128, 384), BF16),
    "residual": ((8, 6144), BF16),
    "gain": ((1, 6144), F32),
    "routes": ((4, 8), jnp.int32),
    "share": ((4, 8), F32),
    "blocks": ((8, 2, 2, 64, 128), BF16),
    "attended": ((2, 64, 384), BF16),
    "partial_in": ((2, 8, 32, 768), BF16),
    "summed": ((8, 8, 768), F32),
    "summed_in": ((8, 8, 768), F32),
    "hidden": ((8, 6144), F32),
    "table": ((2, 8, 1, 128), F32),
    "table1": ((2, 8, 1, 128), F32),
    "table2": ((2, 8, 8, 1, 128), F32),
    "tables": ((2, 8, 8, 1, 128), F32),
    "targets": ((8, 1, 512), F32),
    "gate": ((672, 6144), BF16),
    "up": ((672, 6144), BF16),
    "down": ((2, 672, 6144), BF16),
    "rows": ((2, 3, 4, 4, 4, 2, 16, 512), BF16),
    "relay3": ((3, 2, 4, 2, 2, 16, 512), BF16),
    "full3": ((3, 2, 4, 2, 4, 16, 512), BF16),
    "full2": ((3, 2, 4, 4, 16, 512), BF16),
    "full1": ((3, 2, 4, 16, 512), BF16),
    "selected": ((512, 3072), BF16),
    "sums": ((512, 1536), F32),
    "mixed": ((2, 512, 672), BF16),
    "mixed_other": ((512, 672), BF16),
}
SENDS = {
    "load": (10,),
    "kv": (8,),
    "pair": (8,),
    "weight": (1,),
    "att": (1,),
    "sum": (1,),
    "back": (1,),
    "t1": (1,),
    "t2": (1,),
    "t3": (1,),
    "ag1": (1,),
    "ag2": (1,),
    "ag3": (1,),
    "fwd": (1,),
    "swap": (1,),
    "mix": (1,),
    "rs3": (1,),
    "rs2": (1,),
    "rs1": (1,),
}
RECEIVES = {
    "kv": (8,),
    "pair": (8,),
    "weight": (1,),
    "att": (2,),
    "sum": (2,),
    "back": (1,),
    "t1": (1,),
    "t2": (1,),
    "t3": (1,),
    "ag1": (3,),
    "ag2": (3, 4),
    "ag3": (3, 2, 4, 2),
    "ag3end": (3, 2, 2),
    "fwd": (3, 2),
    "swap": (1,),
    "mix": (1,),
    "rs3": (3, 2, 4, 2),
    "rs3end": (3, 2, 4),
    "rs2": (3, 2),
    "rs1": (3, 2),
}
INPUTS = (
    "query_hbm",
    "kv_hbm",
    "residual_hbm",
    "gain_hbm",
    "routes_hbm",
    "share_hbm",
    "weight_hbm",
    "gate_hbm",
    "up_hbm",
    "down_hbm",
)


def device_at(at):
    return (at["z"] * 2 + at["x"] % 2, at["y"] * 4 + (at["x"] // 2) * 2 + at["k"])


def moved(at, axis, by):
    there = dict(at)
    there[axis] = (at[axis] + by + 4) % 4
    return there


def column_of(h, s, q):
    return h * 3072 + s * 1536 + q * 512


class Links:
    def __init__(self, refs):
        self.refs = refs

    def copy(self, send, receive, source, target, device):
        return pltpu.make_async_remote_copy(
            src_ref=source,
            dst_ref=target,
            send_sem=getattr(self.refs, send[0] + "_s").at[send[1]],
            recv_sem=getattr(self.refs, receive[0] + "_r").at[receive[1]],
            device_id=device,
            device_id_type=MESH,
        )

    def go(self, send, receive, source, target, device):
        self.copy(send, receive, source, target, device).start()

    def arrived(self, name, index, target, device):
        self.copy((next(iter(SENDS)), 0), (name, index), target, target, device).wait_recv()

    def left(self, name, index, source, device):
        self.copy((name, index), (next(iter(RECEIVES)), 0), source, source, device).wait_send()


def row_table(r, links, across, p):
    expert = lax.broadcasted_iota(jnp.int32, (16, 8), 0)
    chosen = jnp.zeros((16, 8), F32)
    share = jnp.zeros((16, 8), F32)
    for t in range(4):
        hit = jnp.where(r.routes[t : t + 1, :] == expert, 1.0, 0.0)
        chosen = chosen + hit
        share = share + hit * r.share[t : t + 1, :]
    upto = jnp.where(
        lax.broadcasted_iota(jnp.int32, (8, 8), 0) <= lax.broadcasted_iota(jnp.int32, (8, 8), 1),
        1.0,
        0.0,
    )
    code = chosen * jnp.dot(chosen, upto, preferred_element_type=F32)
    filled = jnp.concatenate([code, share, jnp.zeros((16, 112), F32)], axis=1)
    for i in range(16):
        r.table[i % 2, i // 2] = filled[i : i + 1]
    r.table1[:, p] = r.table[:, p]
    for i in range(1, 8):
        there = r.table.at[:, (p + i) % 8]
        links.go(("t1", 0), ("t1", 0), there, r.table1.at[:, p], across(i))


def layer_kernel(*refs):
    names = INPUTS + ("out",) + tuple(SCRATCH)
    names += tuple(name + "_s" for name in SENDS)
    names += tuple(name + "_r" for name in RECEIVES)
    r = SimpleNamespace(**dict(zip(names, refs, strict=True)))
    links = Links(r)
    go, arrived, left = links.go, links.arrived, links.left

    c = lax.axis_index("ctx")
    e = lax.axis_index("exp")
    k = e % 2
    p = e // 2
    other = 2 * p + 1 - k
    partner = (c, other)
    at = {"z": c // 2, "x": (p % 2) * 2 + c % 2, "y": e // 4, "k": k}
    near = {(a, d): device_at(moved(at, a, d)) for a in "xyz" for d in (1, -1, 2, -2)}

    def along(j):
        return ((c + j) % 8, e)

    def along_other(j):
        return ((c + j) % 8, other)

    def across(i):
        return (c, 2 * ((p + i) % 8) + k)

    def load(i, source, target):
        copy = pltpu.make_async_copy(source, target, r.load_s.at[i])
        copy.start()
        return copy

    loads = [
        load(0, r.kv_hbm, r.blocks.at[c, k]),
        load(1, r.query_hbm, r.query),
        load(2, r.routes_hbm, r.routes),
        load(3, r.share_hbm, r.share),
        load(4, r.residual_hbm, r.residual),
        load(5, r.gain_hbm, r.gain),
    ]

    barrier = pltpu.get_barrier_semaphore()
    peers = [along(j) for j in range(1, 8)] + [along_other(j) for j in range(8)]
    peers += [across(i) for i in range(1, 8)] + [near["x", 1], near["x", -1]]
    for device in peers:
        pl.semaphore_signal(barrier, inc=1, device_id=device, device_id_type=MESH)
    pl.semaphore_wait(barrier, len(peers))

    loads[0].wait()
    own_block = r.blocks.at[c, k]
    go(("pair", 0), ("pair", 0), own_block, own_block, partner)
    for j in range(1, 8):

        @pl.when(c + j < 8)
        def _(j=j):
            go(("kv", j), ("kv", j), own_block, own_block, along(j))

    def out_weight(side):
        return r.selected.at[pl.ds(0, 384), pl.ds(768 + side * 768, 768)]

    own_weight = load(6, r.weight_hbm, out_weight(k))
    go(("weight", 0), ("weight", 0), r.weight_hbm, out_weight(k), partner)

    loads[2].wait()
    loads[3].wait()
    row_table(r, links, across, p)

    number = lax.broadcasted_iota(jnp.int32, (128, 128), 0)
    position = (number // 8 % 8) * 16 + (number // 64) * 8 + number % 8
    column = lax.broadcasted_iota(jnp.int32, (128, 128), 1)
    reorder = jnp.where(position == column, 1.0, 0.0).astype(BF16)
    loads[1].wait()
    turned = jnp.dot(reorder, r.query[...], preferred_element_type=F32)
    query = jnp.concatenate([turned[:, h * 128 : h * 128 + 128] for h in range(3)], axis=0)
    query = query.astype(BF16)

    for j in range(1, 8):

        @pl.when(c - j >= 0)
        def _(j=j):
            region = r.blocks.at[c - j, k]
            arrived("kv", j, region, along(8 - j))
            go(("pair", j), ("pair", j), region, region, partner)

    big_loads = [
        load(7, r.gate_hbm.at[0], r.gate),
        load(8, r.up_hbm.at[0], r.up),
        load(9, r.down_hbm.at[0], r.down.at[0]),
    ]
    go(("swap", 0), ("swap", 0), r.down_hbm.at[0], r.down.at[1], partner)

    arrived("t1", 0, r.table1.at[:, pl.ds(0, 7)], partner)
    r.table2[:, c] = r.table1[...]
    for j in range(1, 8):
        go(("t2", 0), ("t2", 0), r.table1, r.table2.at[:, c], along(j))

    for j in range(8):
        columns = slice(j * 128, j * 128 + 128)

        @pl.when(c - j >= 0)
        def _(j=j, columns=columns):
            arrived("pair", j, r.blocks.at[c - j, 1 - k], partner)
            keys = jnp.concatenate([r.blocks[c - j, half, 0] for half in range(2)], axis=0)
            score = jnp.dot(query, keys, preferred_element_type=F32) / math.sqrt(HD)
            if j == 0:
                allowed = jnp.concatenate([column <= position] * 3, axis=0)
                score = jnp.where(allowed, score, -1e30)
            r.sums[0:384, columns] = score

        @pl.when(c - j < 0)
        def _(columns=columns):
            r.sums[0:384, columns] = jnp.full((384, 128), -1e30, F32)

    highest = jnp.max(r.sums[0:384, 0:1024], axis=1, keepdims=True)
    r.sums[0:384, 1024:1280] = jnp.zeros((384, 256), F32)
    for j in range(8):

        @pl.when(c - j >= 0)
        def _(j=j):
            now = jnp.exp(r.sums[0:384, j * 128 : j * 128 + 128] - highest)
            values = jnp.concatenate([r.blocks[c - j, half, 1] for half in range(2)], axis=0)
            r.sums[0:384, 1024:1152] += lax.dot_general(
                now.astype(BF16), values, (((1,), (1,)), ((), ())), preferred_element_type=F32
            )
            r.sums[0:384, 1152:1280] += now

    bottom = jnp.sum(r.sums[0:384, 1152:1280], axis=1, keepdims=True)
    result = (r.sums[0:384, 1024:1152] / bottom).astype(BF16)
    for h in range(3):
        for side in range(2):
            start = h * 128 + side * 64
            r.attended[side, :, h * 128 : h * 128 + 128] = result[start : start + 64]

    def gathered(b, side):
        start = pl.multiple_of(b * 64, 64)
        return r.selected.at[pl.ds(start, 64), pl.ds(pl.multiple_of(side * 384, 128), 384)]

    part_of = c // 4
    own_rows = pltpu.make_async_copy(r.attended.at[k], gathered(c, k), r.att_r.at[part_of])
    own_rows.start()
    for j in range(8):
        if j > 0:
            go(("att", 0), ("att", part_of), r.attended.at[k], gathered(c, k), along(j))
        go(("att", 0), ("att", part_of), r.attended.at[1 - k], gathered(c, k), along_other(j))

    arrived("t2", 0, r.table2.at[:, pl.ds(0, 7)], partner)
    r.tables[k] = r.table2[k]
    go(("t3", 0), ("t3", 0), r.table2.at[1 - k], r.tables.at[k], partner)

    own_weight.wait()
    arrived("weight", 0, out_weight(1 - k), partner)

    def partial(i, part):
        return r.selected.at[pl.ds((part * 8 + i) * 32, 32), pl.ds(2304, 768)]

    for part in range(2):
        rows_of = slice(part * 256, part * 256 + 256)
        arrived("att", part, r.selected.at[pl.ds(part * 256, 256), pl.ds(0, 768)], partner)
        value = None
        for side in range(2):
            term = jnp.dot(
                r.selected[rows_of, side * 384 : side * 384 + 384],
                r.selected[0:384, 768 + side * 768 : 1536 + side * 768],
                preferred_element_type=F32,
            )
            value = term if value is None else value + term
        for i in range(8):
            partial(i, part)[...] = jnp.concatenate(
                [value[b * 64 + i * 8 : b * 64 + i * 8 + 8] for b in range(4)], axis=0
            ).astype(BF16)
        for i in range(1, 8):
            go(
                ("sum", 0),
                ("sum", part),
                partial((p + i) % 8, part),
                r.partial_in.at[part, i],
                across(i),
            )
    for part in range(2):
        value = partial(p, part)[...].astype(F32)
        arrived("sum", part, r.partial_in.at[part, pl.ds(1, 7)], partner)
        for i in range(1, 8):
            value = value + r.partial_in[part, i].astype(F32)
        r.summed[part * 4 : part * 4 + 4] = value.reshape(4, 8, 768)
    r.summed_in[c] = r.summed[c]
    for j in range(1, 8):
        go(("back", 0), ("back", 0), r.summed.at[(c + j) % 8], r.summed_in.at[c], along(j))
    loads[4].wait()
    loads[5].wait()
    arrived("back", 0, r.summed_in.at[pl.ds(0, 7)], partner)
    for b in range(8):
        columns = slice(b * 768, b * 768 + 768)
        r.hidden[:, columns] = r.residual[:, columns].astype(F32) + r.summed_in[b]
    hidden = r.hidden[...]
    centered = hidden - jnp.mean(hidden, axis=1, keepdims=True)
    variance = jnp.mean(centered * centered, axis=1, keepdims=True)
    normed = centered * lax.rsqrt(variance + 1e-05) * r.gain[...]

    left("sum", 0, r.partial_in.at[:, pl.ds(0, 7)], partner)

    def ring(axis, by):
        return (at[axis] + by + 4) % 4

    def piece(q, d):
        a1, a2, a3 = ORDERS[q]
        return r.rows.at[k, q, at[a3], at[a2], ring(a1, d)]

    def line(q, d):
        a1, a2, a3 = ORDERS[q]
        return r.rows.at[k, q, at[a3], ring(a2, d)]

    def group(q, s, d, g, side=None):
        a1, a2, a3 = ORDERS[q]
        side = k if side is None else side
        return r.rows.at[side, q, ring(a3, d), ring(a2, g), :, s]

    def half(ref, index):
        return ref.at[pl.ds(index * 2, 2)]

    for q in range(3):
        for s in range(2):
            low, high = column_of(0, s, q), column_of(1, s, q)
            piece(q, 0)[s] = jnp.concatenate(
                [normed[:, low : low + 512], normed[:, high : high + 512]], axis=0
            ).astype(BF16)
        for d in (1, -1, 2):
            go(("ag1", 0), ("ag1", q), piece(q, 0), piece(q, 0), near[ORDERS[q][0], d])

    arrived("t3", 0, r.tables.at[1 - k], partner)
    tables = r.tables[...].reshape(128, 128)
    table_high = tables.astype(BF16)
    table_low = (tables - table_high.astype(F32)).astype(BF16)

    def table_rows(turn, z):
        row = lax.broadcasted_iota(jnp.int32, (32, 128), 0)
        slow, fast = row // 4 % 4, row % 4
        x, y = (slow, fast) if turn else (fast, slow)
        source = row // 16 * 64 + z * 16 + x % 2 * 8 + y * 2 + x // 2
        wanted = source == lax.broadcasted_iota(jnp.int32, (32, 128), 1)
        chooser = jnp.where(wanted, 1.0, 0.0).astype(BF16)
        return jnp.dot(chooser, table_high, preferred_element_type=F32) + jnp.dot(
            chooser, table_low, preferred_element_type=F32
        )

    def pick_targets(turn, z):
        codes = table_rows(turn, z)[:, :8].astype(BF16)
        tile = lax.broadcasted_iota(jnp.int32, (8, 512), 1) % 8
        repeat = jnp.where(tile == lax.broadcasted_iota(jnp.int32, (8, 512), 0), 1.0, 0.0)
        spread = jnp.dot(codes, repeat.astype(BF16), preferred_element_type=F32)
        column = lax.broadcasted_iota(jnp.int32, (32, 512), 1)
        own = column // 16 == lax.broadcasted_iota(jnp.int32, (32, 512), 0)
        code = jnp.sum(jnp.where(own, spread, 0.0), axis=0, keepdims=True)
        column = lax.broadcasted_iota(jnp.int32, (1, 512), 1)
        chip = column // 16 % 16
        if turn:
            chip = chip % 4 * 4 + chip // 4
        base = column // 8 % 2 * 128 + chip * 8 + column // 256 * 4 - 1
        return jnp.where(code > 0, base.astype(F32) + code, -1.0)

    def slot_columns(z):
        found = table_rows(0, z)
        row = lax.broadcasted_iota(jnp.int32, (256, 32), 0)
        repeat = jnp.where(row // 8 == lax.broadcasted_iota(jnp.int32, (256, 32), 1), 1.0, 0.0)
        repeat = repeat.astype(BF16)
        high = found.astype(BF16)
        low = (found - high.astype(F32)).astype(BF16)
        spread = jnp.dot(repeat, high, preferred_element_type=F32) + jnp.dot(
            repeat, low, preferred_element_type=F32
        )
        lane = lax.broadcasted_iota(jnp.int32, (256, 128), 1)
        row = lax.broadcasted_iota(jnp.int32, (256, 128), 0)
        code = jnp.sum(jnp.where(lane == row % 8, spread, 0.0), axis=1, keepdims=True)
        share = jnp.sum(jnp.where(lane == row % 8 + 8, spread, 0.0), axis=1, keepdims=True)
        row = lax.broadcasted_iota(jnp.int32, (256, 1), 0)
        base = row // 8 % 16 * 8 + row // 128 * 4 - 1
        return jnp.where(code > 0, base.astype(F32) + code, -1.0), share

    def forward(q, s, d, g):
        region = group(q, s, d, g)
        go(("fwd", 0), ("fwd", (q, s)), region, region, partner)

    def ring_send(q, s, g):
        for kind, d in ((0, 1), (1, -1)):
            region = group(q, s, 0, g)
            go(("ag3", 0), ("ag3", (q, s, g % 4, kind)), region, region, near[ORDERS[q][2], d])

    def ring_relay(q, s, g):
        for kind, d in ((0, 1), (1, -1)):
            whole = group(q, s, -d, g)
            arrived("ag3", (q, s, g % 4, kind), whole, near[ORDERS[q][2], -d])
            part = half(whole, kind)
            go(("ag3", 0), ("ag3end", (q, s, kind)), part, part, near[ORDERS[q][2], d])
            forward(q, s, -d, g)

    def ring_finish(q, s):
        a1, a2, a3 = ORDERS[q]
        for kind, d in ((0, 1), (1, -1)):
            part = r.rows.at[k, q, ring(a3, 2), :, pl.ds(kind * 2, 2), s]
            arrived("ag3end", (q, s, kind), part, near[a3, -d])
        for g in OFFSETS:
            forward(q, s, 2, g)

    for q in range(3):
        a1, a2, a3 = ORDERS[q]
        arrived("ag1", q, r.rows.at[k, q, at[a3], at[a2], pl.ds(0, 3)], near[a1, 1])
        for d in (1, -1, 2):
            go(("ag2", 0), ("ag2", (q, d % 4)), line(q, 0), line(q, 0), near[a2, d])
        ring_send(q, 0, 0)
        for s in range(2):
            forward(q, s, 0, 0)
    for z in range(4):
        for turn in range(2):
            r.targets[turn * 4 + z] = pick_targets(turn, z)
    for g in (-1, 1, 2):
        for q in range(3):
            arrived("ag2", (q, -g % 4), line(q, g), near[ORDERS[q][1], g])
            ring_send(q, 0, g)
            for s in range(2):
                forward(q, s, 0, g)
    for g in OFFSETS:
        for q in range(3):
            ring_relay(q, 0, g)
    for g in OFFSETS:
        for q in range(3):
            ring_send(q, 1, g)
    for q in range(3):
        ring_finish(q, 0)

    def select(s):
        for q in range(3):
            arrived("fwd", (q, s), r.rows.at[1 - k, q, :, :, :, s], partner)
        slots = lax.broadcasted_iota(jnp.int32, (256, 512), 0).astype(F32)
        for z in range(4):
            for q in range(3):
                picker = jnp.where(slots == r.targets[(4 if q == 1 else 0) + z], 1.0, 0.0)
                sides = []
                for side in range(2):
                    found = (
                        r.rows[side, q, z, :, :, s],
                        r.rows[side, q, :, z, :, s],
                        r.rows[side, q, :, :, z, s],
                    )[q]
                    sides.append(found.reshape(256, 512))
                value = jnp.dot(
                    picker.astype(BF16),
                    jnp.concatenate(sides, axis=0),
                    preferred_element_type=F32,
                ).astype(BF16)
                for h in range(2):
                    start = h * 1536 + q * 512
                    r.selected[z * 128 : z * 128 + 128, start : start + 512] = value[
                        h * 128 : h * 128 + 128
                    ]

    def product(weight, s):
        value = None
        for h in range(2):
            start = column_of(h, s, 0)
            term = lax.dot_general(
                r.selected[:, h * 1536 : h * 1536 + 1536],
                weight[:, start : start + 1536],
                (((1,), (1,)), ((), ())),
                preferred_element_type=F32,
            )
            value = term if value is None else value + term
        return value

    select(0)
    for q in range(3):
        ring_relay(q, 1, 0)
    big_loads[0].wait()
    r.sums[:, 0:672] = product(r.gate, 0)
    for g in (-1, 1):
        for q in range(3):
            ring_relay(q, 1, g)
    big_loads[1].wait()
    r.sums[:, 768:1440] = product(r.up, 0)
    for q in range(3):
        ring_relay(q, 1, 2)
    for q in range(3):
        ring_finish(q, 1)
    select(1)
    r.sums[:, 0:672] += product(r.gate, 1)
    r.sums[:, 768:1440] += product(r.up, 1)

    number = lax.broadcasted_iota(jnp.int32, (256, 128), 1).astype(F32)
    for z in range(4):
        block = slice(z * 128, z * 128 + 128)
        g = r.sums[block, 0:672]
        u = r.sums[block, 768:1440]
        activated = (g / (1.0 + jnp.exp(-g)) * u).astype(BF16)
        place_of, share = slot_columns(z)
        spread = jnp.where(number == place_of, 1.0, 0.0).astype(BF16)
        value = jnp.dot(spread, activated, preferred_element_type=F32) * share
        r.mixed[0, block] = value[:128].astype(BF16)
        r.mixed[1, block] = value[128:].astype(BF16)
        go(
            ("mix", 0),
            ("mix", 0),
            r.mixed.at[1 - k, pl.ds(z * 128, 128)],
            r.mixed_other.at[pl.ds(z * 128, 128)],
            partner,
        )
    big_loads[2].wait()
    left("ag1", 0, r.rows.at[k, :, pl.ds(0, 3), 0, 0], partner)
    left("ag2", 0, r.rows.at[k, :, pl.ds(0, 3), 0], partner)
    left("ag3", 0, r.rows.at[k, :, pl.ds(0, 3)], partner)
    left("fwd", 0, r.rows.at[k], partner)

    def down_unit(q, s):
        sides = []
        for h in range(2):
            start = column_of(h, s, q)
            value = jnp.dot(
                r.mixed[k], r.down[0, :, start : start + 512], preferred_element_type=F32
            )
            if (q, s, h) == (0, 0, 0):
                arrived("mix", 0, r.mixed_other, partner)
                arrived("swap", 0, r.down.at[1], partner)
            value = value + jnp.dot(
                r.mixed_other[...], r.down[1, :, start : start + 512], preferred_element_type=F32
            )
            sides.append(value.reshape(64, 8, 512))
        joined = jnp.concatenate(sides, axis=1).astype(BF16).reshape(4, 4, 4, 16, 512)
        if q == 0:
            r.rows[k, 0, :, :, :, s] = joined
        elif q == 1:
            for x in range(4):
                r.rows[k, 1, x, :, :, s] = joined[:, :, x]
        else:
            for y in range(4):
                for x in range(4):
                    r.rows[k, 2, y, x, :, s] = joined[:, y, x]

    def add_into(ref, *others):
        value = ref[...].astype(F32)
        for other_ref in others:
            value = value + other_ref[...].astype(F32)
        ref[...] = value.astype(BF16)

    def back_first(q, s):
        for g in GROUPS_BACK:
            for kind, d in ((0, 1), (1, -1)):
                go(
                    ("rs3", 0),
                    ("rs3", (q, s, g % 4, kind)),
                    half(group(q, s, 2, g), kind),
                    r.relay3.at[q, s, g % 4, kind],
                    near[ORDERS[q][2], d],
                )

    def back_second(q, s):
        for g in GROUPS_BACK:
            for kind, d in ((0, 1), (1, -1)):
                slot = r.relay3.at[q, s, g % 4, kind]
                arrived("rs3", (q, s, g % 4, kind), slot, near[ORDERS[q][2], -d])
                whole = group(q, s, d, g)
                add_into(half(whole, kind), slot)
                go(
                    ("rs3", 0),
                    ("rs3end", (q, s, g % 4)),
                    whole,
                    r.full3.at[q, s, g % 4, kind],
                    near[ORDERS[q][2], d],
                )

    def back_third(q, s, g):
        slots = [r.full3.at[q, s, g % 4, kind] for kind in range(2)]
        arrived("rs3end", (q, s, g % 4), r.full3.at[q, s, g % 4], partner)
        whole = group(q, s, 0, g)
        add_into(whole, *slots)
        if g != 0:
            slot = r.full2.at[q, s, g % 4]
            go(("rs2", 0), ("rs2", (q, s)), whole, slot, near[ORDERS[q][1], g])

    def back_line(q, s):
        slots = [r.full2.at[q, s, g % 4] for g in (1, -1, 2)]
        arrived("rs2", (q, s), r.full2.at[q, s, pl.ds(1, 3)], partner)
        add_into(group(q, s, 0, 0), *slots)
        for d in (1, -1, 2):
            go(
                ("rs1", 0),
                ("rs1", (q, s)),
                piece(q, d).at[s],
                r.full1.at[q, s, d % 4],
                near[ORDERS[q][0], d],
            )

    def back_end(q, s):
        arrived("rs1", (q, s), r.full1.at[q, s, pl.ds(1, 3)], partner)
        value = piece(q, 0)[s].astype(F32)
        for d in (1, -1, 2):
            value = value + r.full1[q, s, d % 4].astype(F32)
        for h in range(2):
            start = column_of(h, s, q)
            columns = slice(start, start + 512)
            r.out[:, columns] = (r.hidden[:, columns] + value[h * 8 : h * 8 + 8]).astype(BF16)

    for q in range(3):
        down_unit(q, 0)
        back_first(q, 0)
    for q in range(3):
        down_unit(q, 1)
        back_first(q, 1)
        back_second(q, 0)
    for q in range(3):
        back_second(q, 1)
    for s in range(2):
        for g in GROUPS_BACK:
            for q in range(3):
                back_third(q, s, g)
    for s in range(2):
        for q in range(3):
            back_line(q, s)
    for s in range(2):
        for q in range(3):
            back_end(q, s)

    left("rs3", 0, r.rows.at[k, :, pl.ds(0, 3)], partner)
    left("rs2", 0, r.rows.at[k, :, pl.ds(0, 3), 0], partner)
    left("rs1", 0, r.rows.at[k, :, pl.ds(0, 3), 0, 0], partner)
    left("mix", 0, r.mixed_other, partner)
    left("swap", 0, r.down.at[1], partner)
    left("weight", 0, r.weight_hbm, partner)
    left("t1", 0, r.table1.at[:, pl.ds(0, 7)], partner)
    left("t2", 0, r.table2.at[:, pl.ds(0, 7)], partner)
    left("t3", 0, r.table2.at[0], partner)
    left("pair", 0, own_block, partner)
    left("att", 0, r.selected.at[pl.ds(0, 480), pl.ds(0, 768)], partner)
    left("back", 0, r.summed.at[pl.ds(0, 7)], partner)
    for j in range(1, 8):

        @pl.when(c + j < 8)
        def _(j=j):
            left("kv", j, own_block, along(j))

        @pl.when(c - j >= 0)
        def _(j=j):
            left("pair", j, r.blocks.at[c - j, k], partner)


def on_device(
    queries,
    keys_values,
    residual,
    out_weight,
    norm_gain,
    routes,
    route_weight,
    gate_weight,
    up_weight,
    down_weight,
):
    scratch = [pltpu.VMEM(shape, kind) for shape, kind in SCRATCH.values()]
    for shape in [*SENDS.values(), *RECEIVES.values()]:
        scratch.append(pltpu.SemaphoreType.DMA(shape))
    return pl.pallas_call(
        layer_kernel,
        name="layer",
        out_shape=jax.ShapeDtypeStruct(residual.shape, BF16),
        in_specs=[pl.BlockSpec(memory_space=pl.ANY)] * len(INPUTS),
        out_specs=pl.BlockSpec(memory_space=pltpu.VMEM),
        scratch_shapes=scratch,
        compiler_params=pltpu.CompilerParams(
            collective_id=1, has_side_effects=True, vmem_limit_bytes=64 * 1024 * 1024 - 65536
        ),
    )(
        queries,
        keys_values.swapaxes(1, 2),
        residual,
        norm_gain.reshape(1, -1),
        routes.T,
        route_weight.T,
        out_weight,
        gate_weight.swapaxes(1, 2),
        up_weight.swapaxes(1, 2),
        down_weight,
    )


def solution(mesh):
    in_specs = (
        P("ctx", "exp"),
        P(None, "ctx", "exp"),
        P(("ctx", "exp"), None),
        P("exp", "ctx"),
        P(),
        P(("ctx", "exp"), None),
        P(("ctx", "exp"), None),
        P("exp", None, "ctx"),
        P("exp", None, "ctx"),
        P("exp", "ctx", None),
    )
    out_specs = P(("ctx", "exp"), None)
    return jax.shard_map(
        on_device, mesh=mesh, in_specs=in_specs, out_specs=out_specs, check_vma=False
    )
```

```python
import math
from types import SimpleNamespace

import jax
import jax.numpy as jnp
from jax import lax
from jax.experimental import pallas as pl
from jax.experimental.pallas import tpu as pltpu
from jax.sharding import PartitionSpec as P

HD = 128
MESH = pl.DeviceIdType.MESH
BF16 = jnp.bfloat16
F32 = jnp.float32
ORDERS = (("x", "y", "z"), ("y", "z", "x"), ("z", "x", "y"))
OFFSETS = (0, -1, 1, 2)
ROUNDS = 4
WIDTH = 3072 // 3 // ROUNDS

SCRATCH = {
    "query": ((128, 384), BF16),
    "residual": ((8, 6144), BF16),
    "gain": ((1, 6144), F32),
    "routes": ((4, 8), jnp.int32),
    "share": ((4, 8), F32),
    "blocks": ((8, 2, 2, 64, 128), BF16),
    "attended": ((2, 64, 384), BF16),
    "partial_in": ((2, 8, 32, 768), BF16),
    "summed": ((8, 8, 768), F32),
    "summed_in": ((8, 8, 768), F32),
    "hidden": ((8, 6144), F32),
    "table": ((2, 8, 1, 128), F32),
    "table1": ((2, 8, 1, 128), F32),
    "table2": ((2, 8, 8, 1, 128), F32),
    "tables": ((2, 8, 8, 1, 128), F32),
    "targets": ((8, 1, 512), F32),
    "spread": ((2, 4, 256, 128), BF16),
    "gate": ((672, 6144), BF16),
    "up": ((672, 6144), BF16),
    "down": ((2, 672, 6144), BF16),
    "rows": ((2, 3, 4, 4, 4, ROUNDS, 16, WIDTH), BF16),
    "relay3": ((3, ROUNDS, 2, 2, 4, 16, WIDTH), BF16),
    "full3": ((3, ROUNDS, 2, 4, 4, 16, WIDTH), BF16),
    "full2": ((3, ROUNDS, 4, 4, 16, WIDTH), BF16),
    "full1": ((3, ROUNDS, 4, 16, WIDTH), BF16),
    "selected": ((512, 3072), BF16),
    "sums": ((512, 1536), F32),
    "mixed": ((2, 512, 672), BF16),
    "mixed_other": ((512, 672), BF16),
}
SENDS = {
    "load": (10,),
    "kv": (8,),
    "pair": (8,),
    "weight": (1,),
    "att": (1,),
    "sum": (1,),
    "back": (1,),
    "t1": (1,),
    "t2": (1,),
    "t3": (1,),
    "ag1": (1,),
    "ag2": (1,),
    "ag3": (1,),
    "fwd": (1,),
    "swap": (1,),
    "mix": (1,),
    "rs3": (1,),
    "rs2": (1,),
    "rs1": (1,),
}
RECEIVES = {
    "kv": (8,),
    "pair": (8,),
    "weight": (1,),
    "att": (2,),
    "sum": (2,),
    "back": (1,),
    "t1": (1,),
    "t2": (1,),
    "t3": (1,),
    "ag1": (3,),
    "ag2": (3, 4),
    "ag3": (3, ROUNDS, 4, 2),
    "ag3end": (3, ROUNDS, 2),
    "fwd": (3, ROUNDS),
    "fwd0": (3,),
    "swap": (1,),
    "mix": (1,),
    "rs3": (3, ROUNDS, 2),
    "rs3end": (3, ROUNDS),
    "rs2": (3, ROUNDS),
    "rs1": (3, ROUNDS),
}
INPUTS = (
    "query_hbm",
    "kv_hbm",
    "residual_hbm",
    "gain_hbm",
    "routes_hbm",
    "share_hbm",
    "weight_hbm",
    "gate_hbm",
    "up_hbm",
    "down_hbm",
)


def device_at(at):
    return (at["z"] * 2 + at["x"] % 2, at["y"] * 4 + (at["x"] // 2) * 2 + at["k"])


def moved(at, axis, by):
    there = dict(at)
    there[axis] = (at[axis] + by + 4) % 4
    return there


def column_of(h, s, q):
    return h * 3072 + (s * 3 + q) * WIDTH


class Links:
    def __init__(self, refs):
        self.refs = refs

    def copy(self, send, receive, source, target, device):
        return pltpu.make_async_remote_copy(
            src_ref=source,
            dst_ref=target,
            send_sem=getattr(self.refs, send[0] + "_s").at[send[1]],
            recv_sem=getattr(self.refs, receive[0] + "_r").at[receive[1]],
            device_id=device,
            device_id_type=MESH,
        )

    def go(self, send, receive, source, target, device):
        self.copy(send, receive, source, target, device).start()

    def arrived(self, name, index, target, device):
        self.copy((next(iter(SENDS)), 0), (name, index), target, target, device).wait_recv()

    def left(self, name, index, source, device):
        self.copy((name, index), (next(iter(RECEIVES)), 0), source, source, device).wait_send()


def row_table(r, links, across, p):
    expert = lax.broadcasted_iota(jnp.int32, (16, 8), 0)
    chosen = jnp.zeros((16, 8), F32)
    share = jnp.zeros((16, 8), F32)
    for t in range(4):
        hit = jnp.where(r.routes[t : t + 1, :] == expert, 1.0, 0.0)
        chosen = chosen + hit
        share = share + hit * r.share[t : t + 1, :]
    upto = jnp.where(
        lax.broadcasted_iota(jnp.int32, (8, 8), 0) <= lax.broadcasted_iota(jnp.int32, (8, 8), 1),
        1.0,
        0.0,
    )
    code = chosen * jnp.dot(chosen, upto, preferred_element_type=F32)
    filled = jnp.concatenate([code, share, jnp.zeros((16, 112), F32)], axis=1)
    for i in range(16):
        r.table[i % 2, i // 2] = filled[i : i + 1]
    r.table1[:, p] = r.table[:, p]
    for i in range(1, 8):
        there = r.table.at[:, (p + i) % 8]
        links.go(("t1", 0), ("t1", 0), there, r.table1.at[:, p], across(i))


def layer_kernel(*refs):
    names = INPUTS + ("out",) + tuple(SCRATCH)
    names += tuple(name + "_s" for name in SENDS)
    names += tuple(name + "_r" for name in RECEIVES)
    r = SimpleNamespace(**dict(zip(names, refs, strict=True)))
    links = Links(r)
    go, arrived, left = links.go, links.arrived, links.left

    c = lax.axis_index("ctx")
    e = lax.axis_index("exp")
    k = e % 2
    p = e // 2
    other = 2 * p + 1 - k
    partner = (c, other)
    at = {"z": c // 2, "x": (p % 2) * 2 + c % 2, "y": e // 4, "k": k}
    near = {(a, d): device_at(moved(at, a, d)) for a in "xyz" for d in (1, -1, 2, -2)}

    def along(j):
        return ((c + j) % 8, e)

    def along_other(j):
        return ((c + j) % 8, other)

    def across(i):
        return (c, 2 * ((p + i) % 8) + k)

    def load(i, source, target):
        copy = pltpu.make_async_copy(source, target, r.load_s.at[i])
        copy.start()
        return copy

    loads = [
        load(0, r.kv_hbm, r.blocks.at[c, k]),
        load(1, r.query_hbm, r.query),
        load(2, r.routes_hbm, r.routes),
        load(3, r.share_hbm, r.share),
        load(4, r.residual_hbm, r.residual),
        load(5, r.gain_hbm, r.gain),
    ]

    barrier = pltpu.get_barrier_semaphore()
    peers = [along(j) for j in range(1, 8)] + [along_other(j) for j in range(8)]
    peers += [across(i) for i in range(1, 8)] + [near["x", 1], near["x", -1]]
    for device in peers:
        pl.semaphore_signal(barrier, inc=1, device_id=device, device_id_type=MESH)
    pl.semaphore_wait(barrier, len(peers))

    loads[0].wait()
    own_block = r.blocks.at[c, k]
    go(("pair", 0), ("pair", 0), own_block, own_block, partner)
    for j in range(1, 8):

        @pl.when(c + j < 8)
        def _(j=j):
            go(("kv", j), ("kv", j), own_block, own_block, along(j))

    def out_weight(side):
        return r.selected.at[pl.ds(0, 384), pl.ds(768 + side * 768, 768)]

    own_weight = load(6, r.weight_hbm, out_weight(k))
    go(("weight", 0), ("weight", 0), r.weight_hbm, out_weight(k), partner)

    loads[2].wait()
    loads[3].wait()
    row_table(r, links, across, p)

    number = lax.broadcasted_iota(jnp.int32, (128, 128), 0)
    position = (number // 8 % 8) * 16 + (number // 64) * 8 + number % 8
    column = lax.broadcasted_iota(jnp.int32, (128, 128), 1)
    reorder = jnp.where(position == column, 1.0, 0.0).astype(BF16)
    loads[1].wait()
    turned = jnp.dot(reorder, r.query[...], preferred_element_type=F32)
    query = jnp.concatenate([turned[:, h * 128 : h * 128 + 128] for h in range(3)], axis=0)
    query = query.astype(BF16)

    for j in range(1, 8):

        @pl.when(c - j >= 0)
        def _(j=j):
            region = r.blocks.at[c - j, k]
            arrived("kv", j, region, along(8 - j))
            go(("pair", j), ("pair", j), region, region, partner)

    big_loads = [
        load(7, r.gate_hbm.at[0], r.gate),
        load(8, r.up_hbm.at[0], r.up),
        load(9, r.down_hbm.at[0], r.down.at[0]),
    ]
    go(("swap", 0), ("swap", 0), r.down_hbm.at[0], r.down.at[1], partner)

    arrived("t1", 0, r.table1.at[:, pl.ds(0, 7)], partner)
    r.table2[:, c] = r.table1[...]
    for j in range(1, 8):
        go(("t2", 0), ("t2", 0), r.table1, r.table2.at[:, c], along(j))

    for j in range(8):
        columns = slice(j * 128, j * 128 + 128)

        @pl.when(c - j >= 0)
        def _(j=j, columns=columns):
            arrived("pair", j, r.blocks.at[c - j, 1 - k], partner)
            keys = jnp.concatenate([r.blocks[c - j, half, 0] for half in range(2)], axis=0)
            score = jnp.dot(query, keys, preferred_element_type=F32) / math.sqrt(HD)
            if j == 0:
                allowed = jnp.concatenate([column <= position] * 3, axis=0)
                score = jnp.where(allowed, score, -1e30)
            r.sums[0:384, columns] = score

        @pl.when(c - j < 0)
        def _(columns=columns):
            r.sums[0:384, columns] = jnp.full((384, 128), -1e30, F32)

    highest = jnp.max(r.sums[0:384, 0:1024], axis=1, keepdims=True)
    r.sums[0:384, 1024:1280] = jnp.zeros((384, 256), F32)
    for j in range(8):

        @pl.when(c - j >= 0)
        def _(j=j):
            now = jnp.exp(r.sums[0:384, j * 128 : j * 128 + 128] - highest)
            values = jnp.concatenate([r.blocks[c - j, half, 1] for half in range(2)], axis=0)
            r.sums[0:384, 1024:1152] += lax.dot_general(
                now.astype(BF16), values, (((1,), (1,)), ((), ())), preferred_element_type=F32
            )
            r.sums[0:384, 1152:1280] += now

    bottom = jnp.sum(r.sums[0:384, 1152:1280], axis=1, keepdims=True)
    result = (r.sums[0:384, 1024:1152] / bottom).astype(BF16)
    for h in range(3):
        for side in range(2):
            start = h * 128 + side * 64
            r.attended[side, :, h * 128 : h * 128 + 128] = result[start : start + 64]

    def gathered(b, side):
        start = pl.multiple_of(b * 64, 64)
        return r.selected.at[pl.ds(start, 64), pl.ds(pl.multiple_of(side * 384, 128), 384)]

    part_of = c // 4
    own_rows = pltpu.make_async_copy(r.attended.at[k], gathered(c, k), r.att_r.at[part_of])
    own_rows.start()
    for j in range(8):
        if j > 0:
            go(("att", 0), ("att", part_of), r.attended.at[k], gathered(c, k), along(j))
        go(("att", 0), ("att", part_of), r.attended.at[1 - k], gathered(c, k), along_other(j))

    arrived("t2", 0, r.table2.at[:, pl.ds(0, 7)], partner)
    r.tables[k] = r.table2[k]
    go(("t3", 0), ("t3", 0), r.table2.at[1 - k], r.tables.at[k], partner)

    own_weight.wait()
    arrived("weight", 0, out_weight(1 - k), partner)

    def partial(i, part):
        return r.selected.at[pl.ds((part * 8 + i) * 32, 32), pl.ds(2304, 768)]

    for part in range(2):
        rows_of = slice(part * 256, part * 256 + 256)
        arrived("att", part, r.selected.at[pl.ds(part * 256, 256), pl.ds(0, 768)], partner)
        value = None
        for side in range(2):
            term = jnp.dot(
                r.selected[rows_of, side * 384 : side * 384 + 384],
                r.selected[0:384, 768 + side * 768 : 1536 + side * 768],
                preferred_element_type=F32,
            )
            value = term if value is None else value + term
        for i in range(8):
            partial(i, part)[...] = jnp.concatenate(
                [value[b * 64 + i * 8 : b * 64 + i * 8 + 8] for b in range(4)], axis=0
            ).astype(BF16)
        for i in range(1, 8):
            go(
                ("sum", 0),
                ("sum", part),
                partial((p + i) % 8, part),
                r.partial_in.at[part, i],
                across(i),
            )
    arrived("t3", 0, r.tables.at[1 - k], partner)
    tables = r.tables[...].reshape(128, 128)
    table_high = tables.astype(BF16)
    table_low = (tables - table_high.astype(F32)).astype(BF16)

    def table_rows(turn, z):
        row = lax.broadcasted_iota(jnp.int32, (32, 128), 0)
        slow, fast = row // 4 % 4, row % 4
        x, y = (slow, fast) if turn else (fast, slow)
        source = row // 16 * 64 + z * 16 + x % 2 * 8 + y * 2 + x // 2
        wanted = source == lax.broadcasted_iota(jnp.int32, (32, 128), 1)
        chooser = jnp.where(wanted, 1.0, 0.0).astype(BF16)
        return jnp.dot(chooser, table_high, preferred_element_type=F32) + jnp.dot(
            chooser, table_low, preferred_element_type=F32
        )

    def pick_targets(turn, z):
        codes = table_rows(turn, z)[:, :8].astype(BF16)
        tile = lax.broadcasted_iota(jnp.int32, (8, 512), 1) % 8
        repeat = jnp.where(tile == lax.broadcasted_iota(jnp.int32, (8, 512), 0), 1.0, 0.0)
        spread = jnp.dot(codes, repeat.astype(BF16), preferred_element_type=F32)
        column = lax.broadcasted_iota(jnp.int32, (32, 512), 1)
        own = column // 16 == lax.broadcasted_iota(jnp.int32, (32, 512), 0)
        code = jnp.sum(jnp.where(own, spread, 0.0), axis=0, keepdims=True)
        column = lax.broadcasted_iota(jnp.int32, (1, 512), 1)
        chip = column // 16 % 16
        if turn:
            chip = chip % 4 * 4 + chip // 4
        base = column // 8 % 2 * 128 + chip * 8 + column // 256 * 4 - 1
        return jnp.where(code > 0, base.astype(F32) + code, -1.0)

    def slot_columns(z):
        found = table_rows(0, z)
        row = lax.broadcasted_iota(jnp.int32, (256, 32), 0)
        repeat = jnp.where(row // 8 == lax.broadcasted_iota(jnp.int32, (256, 32), 1), 1.0, 0.0)
        repeat = repeat.astype(BF16)
        high = found.astype(BF16)
        low = (found - high.astype(F32)).astype(BF16)
        spread = jnp.dot(repeat, high, preferred_element_type=F32) + jnp.dot(
            repeat, low, preferred_element_type=F32
        )
        lane = lax.broadcasted_iota(jnp.int32, (256, 128), 1)
        row = lax.broadcasted_iota(jnp.int32, (256, 128), 0)
        code = jnp.sum(jnp.where(lane == row % 8, spread, 0.0), axis=1, keepdims=True)
        share = jnp.sum(jnp.where(lane == row % 8 + 8, spread, 0.0), axis=1, keepdims=True)
        row = lax.broadcasted_iota(jnp.int32, (256, 1), 0)
        base = row // 8 % 16 * 8 + row // 128 * 4 - 1
        return jnp.where(code > 0, base.astype(F32) + code, -1.0), share

    for z in range(4):
        for turn in range(2):
            r.targets[turn * 4 + z] = pick_targets(turn, z)
    number = lax.broadcasted_iota(jnp.int32, (256, 128), 1).astype(F32)
    for z in range(4):
        place_of, share = slot_columns(z)
        spread = jnp.where(number == place_of, share, 0.0)
        r.spread[0, z] = spread.astype(BF16)
        r.spread[1, z] = (spread - r.spread[0, z].astype(F32)).astype(BF16)

    for part in range(2):
        value = partial(p, part)[...].astype(F32)
        arrived("sum", part, r.partial_in.at[part, pl.ds(1, 7)], partner)
        for i in range(1, 8):
            value = value + r.partial_in[part, i].astype(F32)
        r.summed[part * 4 : part * 4 + 4] = value.reshape(4, 8, 768)
    r.summed_in[c] = r.summed[c]
    for j in range(1, 8):
        go(("back", 0), ("back", 0), r.summed.at[(c + j) % 8], r.summed_in.at[c], along(j))
    loads[4].wait()
    loads[5].wait()
    arrived("back", 0, r.summed_in.at[pl.ds(0, 7)], partner)
    for b in range(8):
        columns = slice(b * 768, b * 768 + 768)
        r.hidden[:, columns] = r.residual[:, columns].astype(F32) + r.summed_in[b]
    hidden = r.hidden[...]
    centered = hidden - jnp.mean(hidden, axis=1, keepdims=True)
    variance = jnp.mean(centered * centered, axis=1, keepdims=True)
    normed = centered * lax.rsqrt(variance + 1e-05) * r.gain[...]

    left("sum", 0, r.partial_in.at[:, pl.ds(0, 7)], partner)

    def ring(axis, by):
        return (at[axis] + by + 4) % 4

    def piece(q, d):
        a1, a2, a3 = ORDERS[q]
        return r.rows.at[k, q, at[a3], at[a2], ring(a1, d)]

    def line(q, d):
        a1, a2, a3 = ORDERS[q]
        return r.rows.at[k, q, at[a3], ring(a2, d)]

    def group(q, s, d, g, side=None):
        a1, a2, a3 = ORDERS[q]
        side = k if side is None else side
        return r.rows.at[side, q, ring(a3, d), ring(a2, g), :, s]

    def half(ref, index):
        return ref.at[pl.ds(index * 2, 2)]

    for q in range(3):
        for s in range(ROUNDS):
            low, high = column_of(0, s, q), column_of(1, s, q)
            piece(q, 0)[s] = jnp.concatenate(
                [normed[:, low : low + WIDTH], normed[:, high : high + WIDTH]], axis=0
            ).astype(BF16)
        for d in (1, -1, 2):
            go(("ag1", 0), ("ag1", q), piece(q, 0), piece(q, 0), near[ORDERS[q][0], d])

    def plane(q, s, d):
        return r.rows.at[k, q, ring(ORDERS[q][2], d), :, :, s]

    def forward(q, s, d):
        go(("fwd", 0), ("fwd", (q, s)), plane(q, s, d), plane(q, s, d), partner)

    def forward_own(q, g):
        go(("fwd", 0), ("fwd0", q), line(q, g), line(q, g), partner)

    def ring_send(q, s, g):
        for kind, d in ((0, 1), (1, -1)):
            region = group(q, s, 0, g)
            go(("ag3", 0), ("ag3", (q, s, g % 4, kind)), region, region, near[ORDERS[q][2], d])

    def ring_relay(q, s, g):
        for kind, d in ((0, 1), (1, -1)):
            whole = group(q, s, -d, g)
            arrived("ag3", (q, s, g % 4, kind), whole, near[ORDERS[q][2], -d])
            part = half(whole, kind)
            go(("ag3", 0), ("ag3end", (q, s, kind)), part, part, near[ORDERS[q][2], d])
            if g == 2:
                forward(q, s, -d)

    def plane_send(q, s):
        for kind, d in ((0, 1), (1, -1)):
            whole = plane(q, s, 0)
            go(("ag3", 0), ("ag3", (q, s, 0, kind)), whole, whole, near[ORDERS[q][2], d])

    def plane_relay(q, s):
        for kind, d in ((0, 1), (1, -1)):
            whole = plane(q, s, -d)
            arrived("ag3", (q, s, 0, kind), whole, near[ORDERS[q][2], -d])
            part = half(whole, kind)
            go(("ag3", 0), ("ag3end", (q, s, kind)), part, part, near[ORDERS[q][2], d])
            forward(q, s, -d)

    def ring_finish(q, s):
        a1, a2, a3 = ORDERS[q]
        for kind, d in ((0, 1), (1, -1)):
            if s == 0:
                part = r.rows.at[k, q, ring(a3, 2), :, pl.ds(kind * 2, 2), s]
            else:
                part = half(plane(q, s, 2), kind)
            arrived("ag3end", (q, s, kind), part, near[a3, -d])
        forward(q, s, 2)

    for q in range(3):
        a1, a2, a3 = ORDERS[q]
        arrived("ag1", q, r.rows.at[k, q, at[a3], at[a2], pl.ds(0, 3)], near[a1, 1])
        for d in (1, -1, 2):
            go(("ag2", 0), ("ag2", (q, d % 4)), line(q, 0), line(q, 0), near[a2, d])
        ring_send(q, 0, 0)
        forward_own(q, 0)
    for g in (-1, 1, 2):
        for q in range(3):
            arrived("ag2", (q, -g % 4), line(q, g), near[ORDERS[q][1], g])
            ring_send(q, 0, g)
            forward_own(q, g)
    def sends(s):
        if s < ROUNDS:
            for q in range(3):
                plane_send(q, s)

    sends(1)
    for g in OFFSETS:
        for q in range(3):
            ring_relay(q, 0, g)
    sends(2)
    for q in range(3):
        ring_finish(q, 0)

    def select(s):
        for q in range(3):
            if s == 0:
                arrived("fwd0", q, r.rows.at[1 - k, q, 0], partner)
            arrived("fwd", (q, s), r.rows.at[1 - k, q, pl.ds(0, 3), :, :, s], partner)
        slots = lax.broadcasted_iota(jnp.int32, (256, 512), 0).astype(F32)
        for z in range(4):
            for q in range(3):
                picker = jnp.where(slots == r.targets[(4 if q == 1 else 0) + z], 1.0, 0.0)
                sides = []
                for side in range(2):
                    found = (
                        r.rows[side, q, z, :, :, s],
                        r.rows[side, q, :, z, :, s],
                        r.rows[side, q, :, :, z, s],
                    )[q]
                    sides.append(found.reshape(256, WIDTH))
                value = jnp.dot(
                    picker.astype(BF16),
                    jnp.concatenate(sides, axis=0),
                    preferred_element_type=F32,
                ).astype(BF16)
                for h in range(2):
                    start = (h * 3 + q) * WIDTH
                    r.selected[z * 128 : z * 128 + 128, start : start + WIDTH] = value[
                        h * 128 : h * 128 + 128
                    ]

    def product(weight, s):
        value = None
        for h in range(2):
            start = column_of(h, s, 0)
            term = lax.dot_general(
                r.selected[:, h * 3 * WIDTH : h * 3 * WIDTH + 3 * WIDTH],
                weight[:, start : start + 3 * WIDTH],
                (((1,), (1,)), ((), ())),
                preferred_element_type=F32,
            )
            value = term if value is None else value + term
        return value

    for s in range(ROUNDS):
        later = s + 1 < ROUNDS
        select(s)
        if later:
            for q in range(3):
                plane_relay(q, s + 1)
        sends(s + 3)
        if s == 0:
            big_loads[0].wait()
            r.sums[:, 0:672] = product(r.gate, s)
        else:
            r.sums[:, 0:672] += product(r.gate, s)
        if s == 0:
            big_loads[1].wait()
            r.sums[:, 768:1440] = product(r.up, s)
        else:
            r.sums[:, 768:1440] += product(r.up, s)
        if later:
            for q in range(3):
                ring_finish(q, s + 1)

    for z in range(4):
        block = slice(z * 128, z * 128 + 128)
        g = r.sums[block, 0:672]
        u = r.sums[block, 768:1440]
        activated = (g / (1.0 + jnp.exp(-g)) * u).astype(BF16)
        value = jnp.dot(r.spread[0, z], activated, preferred_element_type=F32) + jnp.dot(
            r.spread[1, z], activated, preferred_element_type=F32
        )
        r.mixed[0, block] = value[:128].astype(BF16)
        r.mixed[1, block] = value[128:].astype(BF16)
        go(
            ("mix", 0),
            ("mix", 0),
            r.mixed.at[1 - k, pl.ds(z * 128, 128)],
            r.mixed_other.at[pl.ds(z * 128, 128)],
            partner,
        )
    big_loads[2].wait()
    left("ag1", 0, r.rows.at[k, :, pl.ds(0, 3), 0, 0], partner)
    left("ag2", 0, r.rows.at[k, :, pl.ds(0, 3), 0], partner)
    left("ag3", 0, r.rows.at[k, :, pl.ds(0, 3)], partner)
    left("fwd", 0, r.rows.at[k], partner)

    def down_unit(q, s):
        sides = []
        for h in range(2):
            start = column_of(h, s, q)
            value = jnp.dot(
                r.mixed[k], r.down[0, :, start : start + WIDTH], preferred_element_type=F32
            )
            if (q, s, h) == (0, 0, 0):
                arrived("mix", 0, r.mixed_other, partner)
                arrived("swap", 0, r.down.at[1], partner)
            value = value + jnp.dot(
                r.mixed_other[...], r.down[1, :, start : start + WIDTH], preferred_element_type=F32
            )
            sides.append(value.reshape(64, 8, WIDTH))
        joined = jnp.concatenate(sides, axis=1).astype(BF16).reshape(4, 4, 4, 16, WIDTH)
        if q == 0:
            r.rows[k, 0, :, :, :, s] = joined
        elif q == 1:
            for x in range(4):
                r.rows[k, 1, x, :, :, s] = joined[:, :, x]
        else:
            for y in range(4):
                for x in range(4):
                    r.rows[k, 2, y, x, :, s] = joined[:, y, x]

    def add_into(ref, *others):
        value = ref[...].astype(F32)
        for other_ref in others:
            value = value + other_ref[...].astype(F32)
        ref[...] = value.astype(BF16)

    def back_first(q, s):
        for kind, d in ((0, 1), (1, -1)):
            slot = r.relay3.at[q, s, kind]
            part = half(plane(q, s, 2), kind)
            go(("rs3", 0), ("rs3", (q, s, kind)), part, slot, near[ORDERS[q][2], d])

    def back_second(q, s):
        for kind, d in ((0, 1), (1, -1)):
            slot = r.relay3.at[q, s, kind]
            arrived("rs3", (q, s, kind), slot, near[ORDERS[q][2], -d])
            whole = plane(q, s, d)
            add_into(half(whole, kind), slot)
            target = r.full3.at[q, s, kind]
            go(("rs3", 0), ("rs3end", (q, s)), whole, target, near[ORDERS[q][2], d])

    def back_third(q, s):
        arrived("rs3end", (q, s), r.full3.at[q, s], partner)
        add_into(plane(q, s, 0), r.full3.at[q, s, 0], r.full3.at[q, s, 1])
        for g in (2, 1, -1):
            slot = r.full2.at[q, s, g % 4]
            go(("rs2", 0), ("rs2", (q, s)), group(q, s, 0, g), slot, near[ORDERS[q][1], g])

    def back_line(q, s):
        slots = [r.full2.at[q, s, g % 4] for g in (1, -1, 2)]
        arrived("rs2", (q, s), r.full2.at[q, s, pl.ds(1, 3)], partner)
        add_into(group(q, s, 0, 0), *slots)
        for d in (1, -1, 2):
            go(
                ("rs1", 0),
                ("rs1", (q, s)),
                piece(q, d).at[s],
                r.full1.at[q, s, d % 4],
                near[ORDERS[q][0], d],
            )

    def back_end(q, s):
        arrived("rs1", (q, s), r.full1.at[q, s, pl.ds(1, 3)], partner)
        value = piece(q, 0)[s].astype(F32)
        for d in (1, -1, 2):
            value = value + r.full1[q, s, d % 4].astype(F32)
        for h in range(2):
            start = column_of(h, s, q)
            columns = slice(start, start + WIDTH)
            r.out[:, columns] = (r.hidden[:, columns] + value[h * 8 : h * 8 + 8]).astype(BF16)

    for s in range(ROUNDS + 2):
        for q in range(3):
            if s < ROUNDS:
                down_unit(q, s)
                back_first(q, s)
            if 0 <= s - 1 < ROUNDS:
                back_second(q, s - 1)
        if s >= 2:
            for q in range(3):
                back_third(q, s - 2)
    for s in range(ROUNDS):
        for q in range(3):
            back_line(q, s)
    for s in range(ROUNDS):
        for q in range(3):
            back_end(q, s)

    left("rs3", 0, r.rows.at[k, :, pl.ds(0, 3)], partner)
    left("rs2", 0, r.rows.at[k, :, pl.ds(0, 3), 0], partner)
    left("rs1", 0, r.rows.at[k, :, pl.ds(0, 3), 0, 0], partner)
    left("mix", 0, r.mixed_other, partner)
    left("swap", 0, r.down.at[1], partner)
    left("weight", 0, r.weight_hbm, partner)
    left("t1", 0, r.table1.at[:, pl.ds(0, 7)], partner)
    left("t2", 0, r.table2.at[:, pl.ds(0, 7)], partner)
    left("t3", 0, r.table2.at[0], partner)
    left("pair", 0, own_block, partner)
    left("att", 0, r.selected.at[pl.ds(0, 480), pl.ds(0, 768)], partner)
    left("back", 0, r.summed.at[pl.ds(0, 7)], partner)
    for j in range(1, 8):

        @pl.when(c + j < 8)
        def _(j=j):
            left("kv", j, own_block, along(j))

        @pl.when(c - j >= 0)
        def _(j=j):
            left("pair", j, r.blocks.at[c - j, k], partner)


def on_device(
    queries,
    keys_values,
    residual,
    out_weight,
    norm_gain,
    routes,
    route_weight,
    gate_weight,
    up_weight,
    down_weight,
):
    scratch = [pltpu.VMEM(shape, kind) for shape, kind in SCRATCH.values()]
    for shape in [*SENDS.values(), *RECEIVES.values()]:
        scratch.append(pltpu.SemaphoreType.DMA(shape))
    return pl.pallas_call(
        layer_kernel,
        name="layer",
        out_shape=jax.ShapeDtypeStruct(residual.shape, BF16),
        in_specs=[pl.BlockSpec(memory_space=pl.ANY)] * len(INPUTS),
        out_specs=pl.BlockSpec(memory_space=pltpu.VMEM),
        scratch_shapes=scratch,
        compiler_params=pltpu.CompilerParams(
            collective_id=1, has_side_effects=True, vmem_limit_bytes=64 * 1024 * 1024 - 65536
        ),
    )(
        queries,
        keys_values.swapaxes(1, 2),
        residual,
        norm_gain.reshape(1, -1),
        routes.T,
        route_weight.T,
        out_weight,
        gate_weight.swapaxes(1, 2),
        up_weight.swapaxes(1, 2),
        down_weight,
    )


def solution(mesh):
    in_specs = (
        P("ctx", "exp"),
        P(None, "ctx", "exp"),
        P(("ctx", "exp"), None),
        P("exp", "ctx"),
        P(),
        P(("ctx", "exp"), None),
        P(("ctx", "exp"), None),
        P("exp", None, "ctx"),
        P("exp", None, "ctx"),
        P("exp", "ctx", None),
    )
    out_specs = P(("ctx", "exp"), None)
    return jax.shard_map(
        on_device, mesh=mesh, in_specs=in_specs, out_specs=out_specs, check_vma=False
    )
```
